128 devices in a mesh: lat: 8 (over x, core), lon: 16 (over z, y).
Axes of the slice: x: 4, y: 4, z: 4, core: 2. Of those that a mesh axis runs over, the one named last changes fastest.
Arguments:
- field: bfloat16 [720, 1440, 128], P('lat', 'lon'), may hold values from -6 to 6
- legendre: bfloat16 [720, 720, 720], P('lon', None, 'lat'), may hold values from -0.21875 to 0.21875
- quadrature: float32 [720], P('lat'), may hold values from 0.5 to 2
- mix_real: bfloat16 [720, 128, 128], P('lat'), may hold values from -0.375 to 0.375
- mix_imag: bfloat16 [720, 128, 128], P('lat'), may hold values from -0.375 to 0.375
Outputs:
- output: bfloat16 [720, 1440, 128], P('lat', 'lon')
The draws below stay inside these ranges and needn't reach their ends.
All inputs are finite; a program needn't handle non-finite values.
Results may differ from the reference program's by a relative error of at most 0.015.
Values may be sent and summed in bfloat16 or wider, within the bound.
No kernel may reach another device: no remote copies, remote signals or barrier semaphores. Data moves between devices by JAX's collectives and lax.ppermute only.
A program may use at most 128 MiB of HBM per device.

```python
import math
import jax
import jax.numpy as jnp
from jax import lax

NLAT = 720
NLON = 1440
C = 128
MMAX = 720
LMAX = 720
N_LAT = 8


def shard_levels(key, shape, cuts, smallest, largest):
    def one(position, shards_of):
        heights = jax.random.uniform(jax.random.fold_in(jax.random.fold_in(key, 6), position), (shards_of,), jnp.float32, smallest / len(cuts), largest / len(cuts))
        return jnp.repeat(jnp.exp(heights), shape[position] // shards_of).reshape((-1,) + (1,) * (len(shape) - position - 1))

    gain = one(*cuts[0])
    for cut in cuts[1:]:
        gain = gain * one(*cut)
    return gain


def scatter_about(own_key, dims, deviation, limit, split=(), kind=jnp.bfloat16):
    gain = shard_levels(own_key, dims, split, -0.22, 0.18) if split else 1.0
    entries = jax.random.normal(own_key, dims, jnp.float32) * deviation * gain
    return jnp.minimum(jnp.maximum(entries, -limit), limit).astype(kind)


def setup_inputs(seed: int = 0) -> dict:
    arg_keys = jax.random.split(jax.random.key(seed), 6)
    return {
        "field": scatter_about(arg_keys[0], (NLAT, NLON, C), 1.0, 6.0, ((0, 8), (1, 16))),
        "legendre": scatter_about(arg_keys[1], (MMAX, LMAX, NLAT), NLAT ** -0.5, 0.21875, ((0, 16), (2, 8))),
        "quadrature": jnp.clip(jnp.exp(math.log(2.0) - 1.3862944 * jax.random.uniform(arg_keys[2], (NLAT,), jnp.float32) ** shard_levels(arg_keys[2], (NLAT,), ((0, 8),), -0.2, 0.2)), 0.5, 2.0),
        "mix_real": scatter_about(arg_keys[3], (LMAX, C, C), (2 * C) ** -0.5, 0.375, ((0, 8),)),
        "mix_imag": scatter_about(arg_keys[4], (LMAX, C, C), (2 * C) ** -0.5, 0.375, ((0, 8),)),
    }


def make_tables():
    col_pos = jnp.arange(NLON, dtype=jnp.int32)
    ord_pos = jnp.arange(MMAX, dtype=jnp.int32)
    phase = (col_pos[:, None] * ord_pos[None, :] % NLON).astype(jnp.float32) * (2.0 * jnp.pi / NLON)
    cosine = jnp.cos(phase)
    sine = jnp.sin(phase)
    forward_table = (jnp.stack([cosine, -sine], 1) * (1.0 / jnp.sqrt(jnp.float32(NLON)))).astype(jnp.bfloat16)
    inverse_table = (jnp.stack([cosine.T, -sine.T], 0) * jnp.sqrt(jnp.float32(2.0 / NLON))).astype(jnp.bfloat16)
    return (forward_table, inverse_table)

def reference(field, legendre, quadrature, mix_real, mix_imag):
    forward_table, inverse_table = make_tables()
    fourier = jnp.einsum('anc,nrm->armc', field.astype(jnp.float32), forward_table.astype(jnp.float32)).astype(jnp.bfloat16)
    weighted = (quadrature[:, None, None, None] * fourier.astype(jnp.float32)).astype(jnp.bfloat16)
    degree_pos = jnp.arange(LMAX, dtype=jnp.int32)
    order_pos = jnp.arange(MMAX, dtype=jnp.int32)
    masked = jnp.where(degree_pos[None, :, None] >= order_pos[:, None, None], legendre, jnp.zeros((), jnp.bfloat16))
    band = NLAT // N_LAT

    def forward_one(order):
        table_m = masked[order].reshape(LMAX, N_LAT, band).astype(jnp.float32)
        values_m = weighted[:, :, order, :].reshape(N_LAT, band, 2 * C).astype(jnp.float32)
        partial_sums = jnp.einsum('lba,bak->blk', table_m, values_m).astype(jnp.bfloat16)
        partial_sums = lax.optimization_barrier(partial_sums)
        return lax.optimization_barrier(jnp.sum(partial_sums.astype(jnp.float32), axis=0))
    coefficients = lax.map(forward_one, order_pos)
    coefficients = coefficients.reshape(MMAX, LMAX, 2, C).transpose(1, 2, 0, 3)
    spectral = coefficients.astype(jnp.bfloat16)
    real_part = spectral[:, 0].astype(jnp.float32)
    imag_part = spectral[:, 1].astype(jnp.float32)
    weight_real = mix_real.astype(jnp.float32)
    weight_imag = mix_imag.astype(jnp.float32)

    def apply_mix(values, weights):
        return jnp.einsum('lmc,lcd->lmd', values, weights)
    mixed = jnp.stack([apply_mix(real_part, weight_real) - apply_mix(imag_part, weight_imag), apply_mix(real_part, weight_imag) + apply_mix(imag_part, weight_real)], 1).astype(jnp.bfloat16)

    def inverse_one(order):
        table_m = masked[order]
        values_m = mixed[:, :, order, :].reshape(LMAX, 2 * C)
        return jnp.dot(table_m.T, values_m, preferred_element_type=jnp.float32)
    grid_spectrum = lax.map(inverse_one, order_pos)
    grid_spectrum = grid_spectrum.reshape(MMAX, NLAT, 2, C).transpose(1, 2, 0, 3).astype(jnp.bfloat16)
    synthesis = jnp.einsum('armc,rmn->anc', grid_spectrum.astype(jnp.float32), inverse_table.astype(jnp.float32)).astype(jnp.bfloat16)
    synthesis = lax.optimization_barrier(synthesis)
    return (field.astype(jnp.float32) + synthesis.astype(jnp.float32)).astype(jnp.bfloat16)
```

```python
import jax
import jax.numpy as jnp
import ml_dtypes
import numpy as np
from jax import lax
from jax.experimental import pallas as pl
from jax.experimental.pallas import tpu as pltpu
from jax.sharding import PartitionSpec as P

LAT = 8
LON = 16
ALL = LAT * LON
BAND = 90
PAD = 96
OWN = 6
RM = 2 * OWN
BLOCK = OWN * RM
SPEC = ALL * BLOCK
DEG = 720
DEGPAD = 768
COEF = DEG * RM
PART = BAND * RM
STEP = 15
SHIFTS = (0, 1, 7, 2, 6, 3, 5, 4)
GROUPS = ((4, 3, 5), (2, 6, 1, 7, 0))
SENDS = GROUPS[0] + GROUPS[1]
CH = 128
FULL = 1440
VMEM = 32 * 1024 * 1024
LEGENDRE_VMEM = 58 * 1024 * 1024


def order_of():
    p = np.arange(LAT)[None, :, None]
    q = np.arange(LON)[None, None, :]
    j = np.arange(OWN)[:, None, None]
    first = np.minimum(6 * p, 45 - OWN)
    order = 45 * q + first + j
    valid = np.broadcast_to(first + j >= 6 * p, order.shape)
    return order.reshape(-1), valid.reshape(-1)


def make_tables():
    order, valid = order_of()
    n = np.arange(FULL)
    phase = (n[:, None] * order[None, :] % FULL).astype(np.float32) * np.float32(2.0 * np.pi / FULL)
    cosine = np.cos(phase.astype(np.float64)).astype(np.float32)
    sine = np.sin(phase.astype(np.float64)).astype(np.float32)
    both = np.concatenate([cosine, -sine], 1) * np.concatenate([valid, valid])[None, :]
    both = both.reshape(LON, BAND, 2 * OWN * ALL)
    both = np.pad(both, ((0, 0), (0, PAD - BAND), (0, 0))).reshape(LON * PAD, RM * ALL)
    forward = both * np.float32(1.0 / np.sqrt(np.float32(FULL)))
    inverse = both * np.sqrt(np.float32(2.0 / FULL))
    return (
        np.ascontiguousarray(forward.T).astype(ml_dtypes.bfloat16),
        np.ascontiguousarray(inverse).astype(ml_dtypes.bfloat16),
    )


def widen(src, dst, rows):
    step = 576

    @pl.loop(0, rows // step)
    def _(i):
        part = pl.ds(pl.multiple_of(i * step, step), step)
        dst[part, :] = src[part, :].astype(dst.dtype)


def cut_kernel(scalars_ref, *refs):
    ins, outs = refs[: len(refs) // 2], refs[len(refs) // 2 :]
    count = ins[0].shape[0]
    degree = lax.broadcasted_iota(jnp.int32, (BAND, DEG), 1)
    for s, (in_ref, out_ref) in enumerate(zip(ins, outs)):
        first = scalars_ref[len(ins)] + (scalars_ref[s] + pl.program_id(0)) * count
        out_ref[...] = jnp.zeros(out_ref.shape, out_ref.dtype)
        for j in range(count):
            part = in_ref[j].astype(jnp.float32)
            part = jnp.where(degree >= first + j, part, 0.0)
            out_ref[j, :BAND, :DEG] = part.astype(out_ref.dtype)


def pass_kernel(in_ref, out_ref):
    for i in range(in_ref.shape[0]):
        out_ref[i] = in_ref[i]


def part_of(p):
    return pl.ds(pl.multiple_of(p * PART, 8), PART)


def dft_kernel(quad_ref, x_ref, t_ref, out_ref, s_ref):
    step = pl.program_id(0)
    x = jnp.concatenate(
        [x_ref[:, 0].reshape(LON * PAD, CH), x_ref[:, 1].reshape(LON * PAD, CH)], axis=1
    )
    rows = 768

    @pl.loop(0, RM * ALL // rows)
    def _(chunk):
        t = t_ref[pl.ds(pl.multiple_of(chunk * rows, rows), rows), :]
        y = jnp.dot(t, x, preferred_element_type=jnp.float32)
        for j in range(2):
            a = 2 * step + j
            scaled = y[:, j * CH : (j + 1) * CH] * quad_ref[a]
            for k in range(rows // ALL):
                s_ref[pl.ds(a * RM + chunk * (rows // ALL) + k, ALL, stride=BLOCK), :] = scaled[
                    k * ALL : (k + 1) * ALL
                ]

    @pl.when(step == pl.num_programs(0) - 1)
    def _():
        widen(s_ref, out_ref, SPEC)


def legendre_kernel(src_ref, dest_ref, w_ref, *refs):
    legs, outs, (s_in, s_out) = refs[:LAT], refs[LAT:-2], refs[-2:]
    m = pl.program_id(0)

    @pl.when(m == 0)
    def _():
        widen(w_ref, s_in, SPEC)

    parts = []
    for s in range(LAT):
        base = src_ref[s] * (PAD * RM) + m
        parts.append(
            jnp.concatenate(
                [s_in[pl.ds(base + r * OWN, PAD, stride=RM), :] for r in range(2)], axis=1
            ).astype(jnp.bfloat16)
        )
    w = jnp.concatenate(parts, axis=0)
    leg = jnp.concatenate([leg_ref[0] for leg_ref in legs], axis=0)
    y = lax.dot_general(leg, w, (((0,), (0,)), ((), ())), preferred_element_type=jnp.float32)
    for r in range(2):
        s_out[pl.ds(r * OWN + m, DEG, stride=RM), :] = y[:DEG, r * CH : (r + 1) * CH]

    @pl.when(m == pl.num_programs(0) - 1)
    def _():
        for s, out_ref in enumerate(outs):
            out_ref[...] = s_out[part_of(dest_ref[s]), :].astype(out_ref.dtype)


def mix_kernel(*refs):
    n = (len(refs) - 4) // 2
    xs, (wr_ref, wi_ref), outs = refs[:n], refs[n : n + 2], refs[n + 2 : -2]
    s_in, s_out = refs[-2:]
    step = pl.program_id(0)

    @pl.when(step == 0)
    def _():
        for s, x_ref in enumerate(xs):
            s_in[part_of(s), :] = x_ref[...].astype(s_in.dtype)

    count = wr_ref.shape[0]
    for d in range(count):
        base = (step * count + d) * RM
        x = jnp.concatenate(
            [
                jnp.concatenate(
                    [s_in[pl.ds(base + r * OWN + j, n, stride=PART), :] for j in range(OWN)],
                    axis=0,
                )
                for r in range(2)
            ],
            axis=1,
        ).astype(jnp.bfloat16)
        wr, wi = wr_ref[d], wi_ref[d]
        w = jnp.concatenate(
            [jnp.concatenate([wr, wi], axis=1), jnp.concatenate([-wi, wr], axis=1)], axis=0
        )
        y = jnp.dot(x, w, preferred_element_type=jnp.float32)
        for r in range(2):
            for j in range(OWN):
                s_out[pl.ds(base + r * OWN + j, n, stride=PART), :] = y[
                    j * n : (j + 1) * n, r * CH : (r + 1) * CH
                ]

    @pl.when(step == pl.num_programs(0) - 1)
    def _():
        for s, out_ref in enumerate(outs):
            out_ref[...] = s_out[part_of(s), :].astype(out_ref.dtype)


def inverse_legendre_kernel(src_ref, dest_ref, *refs):
    xs, legs, (out_ref, s_in, s_out) = refs[:LAT], refs[LAT:-3], refs[-3:]
    m = pl.program_id(0)

    @pl.when(m == 0)
    def _():
        for s, x_ref in enumerate(xs):
            s_in[part_of(dest_ref[s]), :] = x_ref[...].astype(s_in.dtype)

    x = jnp.concatenate(
        [s_in[pl.ds(r * OWN + m, DEG, stride=RM), :] for r in range(2)], axis=1
    ).astype(jnp.bfloat16)
    x = jnp.concatenate([x, jnp.zeros((DEGPAD - DEG, 2 * CH), jnp.bfloat16)], axis=0)
    leg = jnp.concatenate([leg_ref[0] for leg_ref in legs], axis=0)
    y = jnp.dot(leg, x, preferred_element_type=jnp.float32)
    for s in range(LAT):
        base = src_ref[s] * (PAD * RM) + m
        for r in range(2):
            s_out[pl.ds(base + r * OWN, PAD, stride=RM), :] = y[
                s * PAD : (s + 1) * PAD, r * CH : (r + 1) * CH
            ]

    @pl.when(m == pl.num_programs(0) - 1)
    def _():
        widen(s_out, out_ref, SPEC)


def inverse_dft_kernel(x_ref, t_ref, out_ref, s_in):
    step = pl.program_id(0)

    @pl.when(step == 0)
    def _():
        widen(x_ref, s_in, SPEC)

    x = jnp.concatenate(
        [
            jnp.concatenate(
                [s_in[pl.ds((2 * step + j) * RM + k, ALL, stride=BLOCK), :] for k in range(RM)],
                axis=0,
            )
            for j in range(2)
        ],
        axis=1,
    ).astype(jnp.bfloat16)
    blocks = 8
    rows = blocks * PAD

    @pl.loop(0, LON // blocks)
    def _(chunk):
        t = t_ref[pl.ds(pl.multiple_of(chunk * rows, rows), rows), :]
        y = jnp.dot(t, x, preferred_element_type=jnp.float32).astype(jnp.bfloat16)
        for j in range(2):
            out_ref[pl.ds(chunk * blocks, blocks), j] = y[:, j * CH : (j + 1) * CH].reshape(
                blocks, PAD, CH
            )


def params(limit=VMEM):
    return pltpu.CompilerParams(dimension_semantics=("arbitrary",), vmem_limit_bytes=limit)


def whole(shape):
    return pl.BlockSpec(shape, lambda *_: (0,) * len(shape))


def cut(table, scalars, n):
    count = 3
    return pl.pallas_call(
        cut_kernel,
        grid_spec=pltpu.PrefetchScalarGridSpec(
            num_scalar_prefetch=1,
            grid=(OWN // count,),
            in_specs=[
                pl.BlockSpec((count, BAND, DEG), lambda i, ref, s=s: (ref[s] + i, 0, 0))
                for s in range(n)
            ],
            out_specs=[pl.BlockSpec((count, PAD, DEGPAD), lambda i, ref: (i, 0, 0))] * n,
        ),
        out_shape=[jax.ShapeDtypeStruct((OWN, PAD, DEGPAD), jnp.bfloat16)] * n,
        compiler_params=params(LEGENDRE_VMEM),
        cost_estimate=pl.CostEstimate(
            flops=1_000_000 * n, bytes_accessed=1_700_000 * n, transcendentals=0
        ),
        name="cut",
    )(scalars, *[table] * n)


def in_order(token):
    return pl.pallas_call(
        pass_kernel,
        in_specs=[pl.BlockSpec(memory_space=pltpu.SMEM)],
        out_specs=pl.BlockSpec(memory_space=pltpu.SMEM),
        out_shape=jax.ShapeDtypeStruct(token.shape, token.dtype),
        cost_estimate=pl.CostEstimate(
            flops=60_000_000_000, bytes_accessed=200_000_000, transcendentals=0
        ),
        name="in_order",
    )(token)


def dft(quad, x, table):
    return pl.pallas_call(
        dft_kernel,
        grid=(OWN // 2,),
        in_specs=[
            pl.BlockSpec(memory_space=pltpu.SMEM),
            pl.BlockSpec((LON, 2, PAD, CH), lambda s: (0, s, 0, 0)),
            whole((RM * ALL, LON * PAD)),
        ],
        out_specs=whole((SPEC, CH)),
        out_shape=jax.ShapeDtypeStruct((SPEC, CH), jnp.bfloat16),
        scratch_shapes=[pltpu.VMEM((SPEC, CH), jnp.float32)],
        compiler_params=params(),
        cost_estimate=pl.CostEstimate(
            flops=1_000_000, bytes_accessed=100_000, transcendentals=0
        ),
        name="dft",
    )(quad, x, table)


def legendre_call(kernel, name, src, dest, xs, legs, rows_out, limit):
    rows_in = [x.shape[0] for x in xs]
    return pl.pallas_call(
        kernel,
        grid=(OWN,),
        in_specs=[pl.BlockSpec(memory_space=pltpu.SMEM)] * 2
        + [whole((rows, CH)) for rows in rows_in]
        + [pl.BlockSpec((1, PAD, DEGPAD), lambda m: (m, 0, 0))] * LAT,
        out_specs=[whole((rows, CH)) for rows in rows_out],
        out_shape=[jax.ShapeDtypeStruct((rows, CH), jnp.bfloat16) for rows in rows_out],
        scratch_shapes=[
            pltpu.VMEM((sum(rows_in), CH), jnp.float32),
            pltpu.VMEM((sum(rows_out), CH), jnp.float32),
        ],
        compiler_params=params(limit),
        cost_estimate=pl.CostEstimate(
            flops=2 * 6 * 768 * 768 * 256, bytes_accessed=12_000_000, transcendentals=0
        ),
        name=name,
    )(src, dest, *xs, *legs)


def mix(xs, wr, wi):
    n = len(xs)
    weight = pl.BlockSpec((STEP, CH, CH), lambda s: (s, 0, 0))
    return pl.pallas_call(
        mix_kernel,
        grid=(BAND // STEP,),
        in_specs=[whole((PART, CH))] * n + [weight, weight],
        out_specs=[whole((PART, CH))] * n,
        out_shape=[jax.ShapeDtypeStruct((PART, CH), jnp.bfloat16)] * n,
        scratch_shapes=[pltpu.VMEM((n * PART, CH), jnp.float32)] * 2,
        compiler_params=params(),
        cost_estimate=pl.CostEstimate(
            flops=2 * 90 * 48 * 256 * 256, bytes_accessed=10_000_000, transcendentals=0
        ),
        name="mix",
    )(*xs, wr, wi)


def inverse_dft(x, table):
    return pl.pallas_call(
        inverse_dft_kernel,
        grid=(OWN // 2,),
        in_specs=[whole((SPEC, CH)), whole((LON * PAD, RM * ALL))],
        out_specs=pl.BlockSpec((LON, 2, PAD, CH), lambda s: (0, s, 0, 0)),
        out_shape=jax.ShapeDtypeStruct((LON, OWN, PAD, CH), jnp.bfloat16),
        scratch_shapes=[pltpu.VMEM((SPEC, CH), jnp.float32)],
        compiler_params=params(),
        cost_estimate=pl.CostEstimate(
            flops=2 * 1536 * 1536 * 768, bytes_accessed=10_000_000, transcendentals=0
        ),
        name="inverse_dft",
    )(x, table)


def swap(x, axes):
    return lax.all_to_all(x, axes, split_axis=0, concat_axis=0, tiled=True)


def shifted(part, shift):
    if shift == 0:
        return part
    return lax.ppermute(part, "lat", [(i, (i + shift) % LAT) for i in range(LAT)])


def per_device(field, legendre, quadrature, mix_real, mix_imag):
    p = lax.axis_index("lat")
    q = lax.axis_index("lon")
    forward_table, inverse_table = make_tables()

    rows = swap(jnp.pad(field, ((0, PAD - BAND), (0, PAD - BAND), (0, 0))), "lon")

    orders = legendre.shape[0]
    table = jnp.transpose(legendre, (0, 2, 1))
    shifts = jnp.array(SHIFTS, jnp.int32)
    firsts = jnp.minimum(lax.rem(p + shifts, LAT) * (OWN // 3), (orders - OWN) // 3)
    src = lax.rem(p - shifts + LAT, LAT)
    dest = lax.rem(p + jnp.array(SENDS, jnp.int32), LAT)
    cuts = [None] * LAT
    for group in ((1, 2, 3, 4), (5, 6, 7, 0)):
        scalars = jnp.stack([firsts[i] for i in group] + [q * orders])
        parts = cut(table, scalars, len(group))
        table, *parts = lax.optimization_barrier((table, *parts))
        for i, part in zip(group, parts):
            cuts[i] = part
    quad = lax.dynamic_slice_in_dim(jnp.pad(quadrature, (0, PAD - BAND)), q * OWN, OWN, 0)

    legs = list(cuts)

    def end(value, places):
        parts = [shifted(cuts[i], SHIFTS[i]) for i in places]
        value, parts = lax.optimization_barrier((value, parts))
        for i, part in zip(places, parts):
            legs[i] = part
        return value

    dest = in_order(end(dest, (1, 2, 3, 4, 7)))
    cuts[5:7], rows, dest = lax.optimization_barrier((cuts[5:7], rows, dest))
    spectrum = dft(quad, rows.reshape(LON, OWN, PAD, CH), jnp.asarray(forward_table))
    dest = in_order(end(dest, (5, 6)))
    weighted = swap(spectrum, ("lat", "lon"))
    coefficients = legendre_call(
        legendre_kernel, "legendre", src, dest, [weighted], legs, [PART] * LAT, LEGENDRE_VMEM
    )
    mixed = []
    for group in GROUPS:
        parts = [shifted(coefficients[len(mixed) + i], shift) for i, shift in enumerate(group)]
        parts = mix(parts, mix_real, mix_imag)
        mixed += [shifted(part, (LAT - shift) % LAT) for part, shift in zip(parts, group)]
    (grid_spectrum,) = legendre_call(
        inverse_legendre_kernel, "inverse_legendre", src, dest, mixed, legs, [SPEC], VMEM
    )
    grid_spectrum = swap(grid_spectrum, ("lat", "lon"))
    samples = inverse_dft(grid_spectrum, jnp.asarray(inverse_table))
    synthesis = swap(samples.reshape(LON * OWN, PAD, CH), "lon")[:BAND, :BAND]
    return (field.astype(jnp.float32) + synthesis.astype(jnp.float32)).astype(jnp.bfloat16)


def solution(mesh):
    placed = (
        P("lat", "lon", None),
        P("lon", None, "lat"),
        P("lat"),
        P("lat", None, None),
        P("lat", None, None),
    )
    return jax.shard_map(
        per_device, mesh=mesh, in_specs=placed, out_specs=P("lat", "lon", None), check_vma=False
    )
```

```python
import jax
import jax.numpy as jnp
import ml_dtypes
import numpy as np
from jax import lax
from jax.experimental import pallas as pl
from jax.experimental.pallas import tpu as pltpu
from jax.sharding import PartitionSpec as P

LAT = 8
LON = 16
ALL = LAT * LON
BAND = 90
PAD = 96
OWN = 6
RM = 2 * OWN
BLOCK = OWN * RM
SPEC = ALL * BLOCK
DEG = 720
DEGPAD = 768
COEF = DEG * RM
PART = BAND * RM
STEP = 15
SHIFTS = (0, 1, 7, 2, 6, 3, 5, 4)
GROUPS = ((4, 3, 5), (2, 6, 1, 7, 0))
SENDS = GROUPS[0] + GROUPS[1]
CH = 128
FULL = 1440
VMEM = 24 * 1024 * 1024
CUT_VMEM = 58 * 1024 * 1024


def order_of():
    p = np.arange(LAT)[None, :, None]
    q = np.arange(LON)[None, None, :]
    j = np.arange(OWN)[:, None, None]
    first = np.minimum(6 * p, 45 - OWN)
    order = 45 * q + first + j
    valid = np.broadcast_to(first + j >= 6 * p, order.shape)
    return order.reshape(-1), valid.reshape(-1)


def make_tables():
    order, valid = order_of()
    n = np.arange(FULL)
    phase = (n[:, None] * order[None, :] % FULL).astype(np.float32) * np.float32(2.0 * np.pi / FULL)
    cosine = np.cos(phase.astype(np.float64)).astype(np.float32)
    sine = np.sin(phase.astype(np.float64)).astype(np.float32)
    both = np.concatenate([cosine, -sine], 1) * np.concatenate([valid, valid])[None, :]
    both = both.reshape(LON, BAND, 2 * OWN * ALL)
    both = np.pad(both, ((0, 0), (0, PAD - BAND), (0, 0))).reshape(LON * PAD, RM * ALL)
    forward = both * np.float32(1.0 / np.sqrt(np.float32(FULL)))
    inverse = both * np.sqrt(np.float32(2.0 / FULL))
    return (
        np.ascontiguousarray(forward.T).astype(ml_dtypes.bfloat16),
        np.ascontiguousarray(inverse).astype(ml_dtypes.bfloat16),
    )


def widen(src, dst, rows):
    step = 576

    @pl.loop(0, rows // step)
    def _(i):
        part = pl.ds(pl.multiple_of(i * step, step), step)
        dst[part, :] = src[part, :].astype(dst.dtype)


def cut_kernel(scalars_ref, *refs):
    ins, outs = refs[: len(refs) // 2], refs[len(refs) // 2 :]
    count = ins[0].shape[0]
    degree = lax.broadcasted_iota(jnp.int32, (BAND, DEG), 1)
    for s, (in_ref, out_ref) in enumerate(zip(ins, outs)):
        first = scalars_ref[len(ins)] + (scalars_ref[s] + pl.program_id(0)) * count
        out_ref[...] = jnp.zeros(out_ref.shape, out_ref.dtype)
        for j in range(count):
            part = in_ref[j].astype(jnp.float32)
            part = jnp.where(degree >= first + j, part, 0.0)
            out_ref[j, :BAND, :DEG] = part.astype(out_ref.dtype)


def pass_kernel(in_ref, out_ref):
    for i in range(in_ref.shape[0]):
        out_ref[i] = in_ref[i]


def part_of(p):
    return pl.ds(pl.multiple_of(p * PART, 8), PART)


def dft_kernel(quad_ref, x_ref, t_ref, out_ref, s_ref):
    step = pl.program_id(0)
    x = jnp.concatenate(
        [x_ref[:, 0].reshape(LON * PAD, CH), x_ref[:, 1].reshape(LON * PAD, CH)], axis=1
    )
    rows = 768

    @pl.loop(0, RM * ALL // rows)
    def _(chunk):
        t = t_ref[pl.ds(pl.multiple_of(chunk * rows, rows), rows), :]
        y = jnp.dot(t, x, preferred_element_type=jnp.float32)
        for j in range(2):
            a = 2 * step + j
            scaled = y[:, j * CH : (j + 1) * CH] * quad_ref[a]
            for k in range(rows // ALL):
                s_ref[pl.ds(a * RM + chunk * (rows // ALL) + k, ALL, stride=BLOCK), :] = scaled[
                    k * ALL : (k + 1) * ALL
                ]

    @pl.when(step == pl.num_programs(0) - 1)
    def _():
        widen(s_ref, out_ref, SPEC)


def legendre_kernel(src_ref, dest_ref, w_ref, *refs):
    legs, outs, (s_in, s_out) = refs[:LAT], refs[LAT:-2], refs[-2:]
    m = pl.program_id(0)

    @pl.when(m == 0)
    def _():
        widen(w_ref, s_in, SPEC)

    parts = []
    for s in range(LAT):
        base = src_ref[s] * (PAD * RM) + m
        parts.append(
            jnp.concatenate(
                [s_in[pl.ds(base + r * OWN, PAD, stride=RM), :] for r in range(2)], axis=1
            ).astype(jnp.bfloat16)
        )
    w = jnp.concatenate(parts, axis=0)
    leg = jnp.concatenate([leg_ref[0] for leg_ref in legs], axis=0)
    y = lax.dot_general(leg, w, (((0,), (0,)), ((), ())), preferred_element_type=jnp.float32)
    for r in range(2):
        s_out[pl.ds(r * OWN + m, DEG, stride=RM), :] = y[:DEG, r * CH : (r + 1) * CH]

    @pl.when(m == pl.num_programs(0) - 1)
    def _():
        for s, out_ref in enumerate(outs):
            out_ref[...] = s_out[part_of(dest_ref[s]), :].astype(out_ref.dtype)


def mix_kernel(*refs):
    n = (len(refs) - 4) // 2
    xs, (wr_ref, wi_ref), outs = refs[:n], refs[n : n + 2], refs[n + 2 : -2]
    s_in, s_out = refs[-2:]
    step = pl.program_id(0)

    @pl.when(step == 0)
    def _():
        for s, x_ref in enumerate(xs):
            s_in[part_of(s), :] = x_ref[...].astype(s_in.dtype)

    count = wr_ref.shape[0]
    for d in range(count):
        base = (step * count + d) * RM
        x = jnp.concatenate(
            [
                jnp.concatenate(
                    [s_in[pl.ds(base + r * OWN + j, n, stride=PART), :] for j in range(OWN)],
                    axis=0,
                )
                for r in range(2)
            ],
            axis=1,
        ).astype(jnp.bfloat16)
        wr, wi = wr_ref[d], wi_ref[d]
        w = jnp.concatenate(
            [jnp.concatenate([wr, wi], axis=1), jnp.concatenate([-wi, wr], axis=1)], axis=0
        )
        y = jnp.dot(x, w, preferred_element_type=jnp.float32)
        for r in range(2):
            for j in range(OWN):
                s_out[pl.ds(base + r * OWN + j, n, stride=PART), :] = y[
                    j * n : (j + 1) * n, r * CH : (r + 1) * CH
                ]

    @pl.when(step == pl.num_programs(0) - 1)
    def _():
        for s, out_ref in enumerate(outs):
            out_ref[...] = s_out[part_of(s), :].astype(out_ref.dtype)


def inverse_legendre_kernel(src_ref, dest_ref, *refs):
    xs, legs, (out_ref, s_in, s_out) = refs[:LAT], refs[LAT:-3], refs[-3:]
    m = pl.program_id(0)

    @pl.when(m == 0)
    def _():
        for s, x_ref in enumerate(xs):
            s_in[part_of(dest_ref[s]), :] = x_ref[...].astype(s_in.dtype)

    x = jnp.concatenate(
        [s_in[pl.ds(r * OWN + m, DEG, stride=RM), :] for r in range(2)], axis=1
    ).astype(jnp.bfloat16)
    x = jnp.concatenate([x, jnp.zeros((DEGPAD - DEG, 2 * CH), jnp.bfloat16)], axis=0)
    leg = jnp.concatenate([leg_ref[0] for leg_ref in legs], axis=0)
    y = jnp.dot(leg, x, preferred_element_type=jnp.float32)
    for s in range(LAT):
        base = src_ref[s] * (PAD * RM) + m
        for r in range(2):
            s_out[pl.ds(base + r * OWN, PAD, stride=RM), :] = y[
                s * PAD : (s + 1) * PAD, r * CH : (r + 1) * CH
            ]

    @pl.when(m == pl.num_programs(0) - 1)
    def _():
        widen(s_out, out_ref, SPEC)


def inverse_dft_kernel(x_ref, t_ref, out_ref, s_in):
    step = pl.program_id(0)

    @pl.when(step == 0)
    def _():
        widen(x_ref, s_in, SPEC)

    x = jnp.concatenate(
        [
            jnp.concatenate(
                [s_in[pl.ds((2 * step + j) * RM + k, ALL, stride=BLOCK), :] for k in range(RM)],
                axis=0,
            )
            for j in range(2)
        ],
        axis=1,
    ).astype(jnp.bfloat16)
    blocks = 8
    rows = blocks * PAD

    @pl.loop(0, LON // blocks)
    def _(chunk):
        t = t_ref[pl.ds(pl.multiple_of(chunk * rows, rows), rows), :]
        y = jnp.dot(t, x, preferred_element_type=jnp.float32).astype(jnp.bfloat16)
        for j in range(2):
            out_ref[pl.ds(chunk * blocks, blocks), j] = y[:, j * CH : (j + 1) * CH].reshape(
                blocks, PAD, CH
            )


def params(limit=VMEM):
    return pltpu.CompilerParams(dimension_semantics=("arbitrary",), vmem_limit_bytes=limit)


def whole(shape):
    return pl.BlockSpec(shape, lambda *_: (0,) * len(shape))


def cut(table, scalars, n):
    count = 3
    return pl.pallas_call(
        cut_kernel,
        grid_spec=pltpu.PrefetchScalarGridSpec(
            num_scalar_prefetch=1,
            grid=(OWN // count,),
            in_specs=[
                pl.BlockSpec((count, BAND, DEG), lambda i, ref, s=s: (ref[s] + i, 0, 0))
                for s in range(n)
            ],
            out_specs=[pl.BlockSpec((count, PAD, DEGPAD), lambda i, ref: (i, 0, 0))] * n,
        ),
        out_shape=[jax.ShapeDtypeStruct((OWN, PAD, DEGPAD), jnp.bfloat16)] * n,
        compiler_params=params(CUT_VMEM),
        cost_estimate=pl.CostEstimate(
            flops=1_000_000 * n, bytes_accessed=1_700_000 * n, transcendentals=0
        ),
        name="cut",
    )(scalars, *[table] * n)


def in_order(token):
    return pl.pallas_call(
        pass_kernel,
        in_specs=[pl.BlockSpec(memory_space=pltpu.SMEM)],
        out_specs=pl.BlockSpec(memory_space=pltpu.SMEM),
        out_shape=jax.ShapeDtypeStruct(token.shape, token.dtype),
        compiler_params=pltpu.CompilerParams(vmem_limit_bytes=1024 * 1024),
        cost_estimate=pl.CostEstimate(
            flops=60_000_000_000, bytes_accessed=200_000_000, transcendentals=0
        ),
        name="in_order",
    )(token)


def dft(quad, x, table):
    return pl.pallas_call(
        dft_kernel,
        grid=(OWN // 2,),
        in_specs=[
            pl.BlockSpec(memory_space=pltpu.SMEM),
            pl.BlockSpec((LON, 2, PAD, CH), lambda s: (0, s, 0, 0)),
            whole((RM * ALL, LON * PAD)),
        ],
        out_specs=whole((SPEC, CH)),
        out_shape=jax.ShapeDtypeStruct((SPEC, CH), jnp.bfloat16),
        scratch_shapes=[pltpu.VMEM((SPEC, CH), jnp.float32)],
        compiler_params=params(),
        cost_estimate=pl.CostEstimate(
            flops=1_000_000, bytes_accessed=100_000, transcendentals=0
        ),
        name="dft",
    )(quad, x, table)


def legendre_call(kernel, name, src, dest, xs, legs, rows_out, limit):
    rows_in = [x.shape[0] for x in xs]
    return pl.pallas_call(
        kernel,
        grid=(OWN,),
        in_specs=[pl.BlockSpec(memory_space=pltpu.SMEM)] * 2
        + [whole((rows, CH)) for rows in rows_in]
        + [pl.BlockSpec((1, PAD, DEGPAD), lambda m: (m, 0, 0))] * LAT,
        out_specs=[whole((rows, CH)) for rows in rows_out],
        out_shape=[jax.ShapeDtypeStruct((rows, CH), jnp.bfloat16) for rows in rows_out],
        scratch_shapes=[
            pltpu.VMEM((sum(rows_in), CH), jnp.float32),
            pltpu.VMEM((sum(rows_out), CH), jnp.float32),
        ],
        compiler_params=params(limit),
        cost_estimate=pl.CostEstimate(
            flops=2 * 6 * 768 * 768 * 256, bytes_accessed=12_000_000, transcendentals=0
        ),
        name=name,
    )(src, dest, *xs, *legs)


def mix(xs, wr, wi):
    n = len(xs)
    weight = pl.BlockSpec((STEP, CH, CH), lambda s: (s, 0, 0))
    return pl.pallas_call(
        mix_kernel,
        grid=(BAND // STEP,),
        in_specs=[whole((PART, CH))] * n + [weight, weight],
        out_specs=[whole((PART, CH))] * n,
        out_shape=[jax.ShapeDtypeStruct((PART, CH), jnp.bfloat16)] * n,
        scratch_shapes=[pltpu.VMEM((n * PART, CH), jnp.float32)] * 2,
        compiler_params=params(),
        cost_estimate=pl.CostEstimate(
            flops=2 * 90 * 48 * 256 * 256, bytes_accessed=10_000_000, transcendentals=0
        ),
        name="mix",
    )(*xs, wr, wi)


def inverse_dft(x, table):
    return pl.pallas_call(
        inverse_dft_kernel,
        grid=(OWN // 2,),
        in_specs=[whole((SPEC, CH)), whole((LON * PAD, RM * ALL))],
        out_specs=pl.BlockSpec((LON, 2, PAD, CH), lambda s: (0, s, 0, 0)),
        out_shape=jax.ShapeDtypeStruct((LON, OWN, PAD, CH), jnp.bfloat16),
        scratch_shapes=[pltpu.VMEM((SPEC, CH), jnp.float32)],
        compiler_params=params(),
        cost_estimate=pl.CostEstimate(
            flops=2 * 1536 * 1536 * 768, bytes_accessed=10_000_000, transcendentals=0
        ),
        name="inverse_dft",
    )(x, table)


def swap(x, axes):
    return lax.all_to_all(x, axes, split_axis=0, concat_axis=0, tiled=True)


def shifted(part, shift):
    if shift == 0:
        return part
    return lax.ppermute(part, "lat", [(i, (i + shift) % LAT) for i in range(LAT)])


def per_device(field, legendre, quadrature, mix_real, mix_imag):
    p = lax.axis_index("lat")
    q = lax.axis_index("lon")
    forward_table, inverse_table = make_tables()

    rows = swap(jnp.pad(field, ((0, PAD - BAND), (0, PAD - BAND), (0, 0))), "lon")

    orders = legendre.shape[0]
    table = jnp.transpose(legendre, (0, 2, 1))
    shifts = jnp.array(SHIFTS, jnp.int32)
    src = lax.rem(p - shifts + LAT, LAT)
    dest = lax.rem(p + jnp.array(SENDS, jnp.int32), LAT)
    cuts = [None] * LAT
    for group in ((1, 2, 3, 4), (5, 6, 7, 0)):
        moves = jnp.array([SHIFTS[i] for i in group] + [0], jnp.int32)
        firsts = jnp.minimum(lax.rem(p + moves, LAT) * (OWN // 3), (orders - OWN) // 3)
        scalars = jnp.where(jnp.arange(len(group) + 1) == len(group), q * orders, firsts)
        parts = cut(table, scalars, len(group))
        table, *parts = lax.optimization_barrier((table, *parts))
        for i, part in zip(group, parts):
            cuts[i] = part
    quad = lax.dynamic_slice_in_dim(jnp.pad(quadrature, (0, PAD - BAND)), q * OWN, OWN, 0)

    legs = list(cuts)

    def end(value, places):
        parts = [shifted(cuts[i], SHIFTS[i]) for i in places]
        value, parts = lax.optimization_barrier((value, parts))
        for i, part in zip(places, parts):
            legs[i] = part
        return value

    dest = in_order(end(dest, (1, 2, 3, 4, 7)))
    cuts[5:7], rows, dest = lax.optimization_barrier((cuts[5:7], rows, dest))
    spectrum = dft(quad, rows.reshape(LON, OWN, PAD, CH), jnp.asarray(forward_table))
    dest = in_order(end(dest, (5, 6)))
    weighted = swap(spectrum, ("lat", "lon"))
    coefficients = legendre_call(
        legendre_kernel, "legendre", src, dest, [weighted], legs, [PART] * LAT, VMEM
    )
    mixed = []
    for group in GROUPS:
        parts = [shifted(coefficients[len(mixed) + i], shift) for i, shift in enumerate(group)]
        parts = mix(parts, mix_real, mix_imag)
        mixed += [shifted(part, (LAT - shift) % LAT) for part, shift in zip(parts, group)]
    (grid_spectrum,) = legendre_call(
        inverse_legendre_kernel, "inverse_legendre", src, dest, mixed, legs, [SPEC], VMEM
    )
    grid_spectrum = swap(grid_spectrum, ("lat", "lon"))
    samples = inverse_dft(grid_spectrum, jnp.asarray(inverse_table))
    synthesis = swap(samples.reshape(LON * OWN, PAD, CH), "lon")[:BAND, :BAND]
    return (field.astype(jnp.float32) + synthesis.astype(jnp.float32)).astype(jnp.bfloat16)


def solution(mesh):
    placed = (
        P("lat", "lon", None),
        P("lon", None, "lat"),
        P("lat"),
        P("lat", None, None),
        P("lat", None, None),
    )
    return jax.shard_map(
        per_device, mesh=mesh, in_specs=placed, out_specs=P("lat", "lon", None), check_vma=False
    )
```

```python
import functools

import jax
import jax.numpy as jnp
import ml_dtypes
import numpy as np
from jax import lax
from jax.experimental import pallas as pl
from jax.experimental.pallas import tpu as pltpu
from jax.sharding import PartitionSpec as P

LAT = 8
LON = 16
ALL = LAT * LON
BAND = 90
PAD = 96
OWN = 6
RM = 2 * OWN
BLOCK = OWN * RM
SPEC = ALL * BLOCK
DEG = 720
DEGPAD = 768
COEF = DEG * RM
PART = BAND * RM
STEP = 15
SHIFTS = (0, 1, 7, 2, 6, 3, 5, 4)
GROUPS = ((4, 3, 5), (2, 6, 1, 7, 0))
SENDS = GROUPS[0] + GROUPS[1]
CH = 128
FULL = 1440
VMEM = 24 * 1024 * 1024
CUT_VMEM = 58 * 1024 * 1024


def order_of():
    p = np.arange(LAT)[None, :, None]
    q = np.arange(LON)[None, None, :]
    j = np.arange(OWN)[:, None, None]
    first = np.minimum(6 * p, 45 - OWN)
    order = 45 * q + first + j
    valid = np.broadcast_to(first + j >= 6 * p, order.shape)
    return order.reshape(-1), valid.reshape(-1)


def make_tables():
    order, valid = order_of()
    n = np.arange(FULL)
    phase = (n[:, None] * order[None, :] % FULL).astype(np.float32) * np.float32(2.0 * np.pi / FULL)
    cosine = np.cos(phase.astype(np.float64)).astype(np.float32)
    sine = np.sin(phase.astype(np.float64)).astype(np.float32)
    both = np.concatenate([cosine, -sine], 1) * np.concatenate([valid, valid])[None, :]
    both = both.reshape(LON, BAND, 2 * OWN * ALL)
    both = np.pad(both, ((0, 0), (0, PAD - BAND), (0, 0))).reshape(LON * PAD, RM * ALL)
    forward = both * np.float32(1.0 / np.sqrt(np.float32(FULL)))
    inverse = both * np.sqrt(np.float32(2.0 / FULL))
    return (
        np.ascontiguousarray(forward.T).astype(ml_dtypes.bfloat16),
        np.ascontiguousarray(inverse).astype(ml_dtypes.bfloat16),
    )


def widen(src, dst, rows):
    step = 576

    @pl.loop(0, rows // step)
    def _(i):
        part = pl.ds(pl.multiple_of(i * step, step), step)
        dst[part, :] = src[part, :].astype(dst.dtype)


def cut_kernel(places, scalars_ref, *refs):
    ins, outs = refs[: len(refs) // 2], refs[len(refs) // 2 :]
    count = ins[0].shape[0]
    degree = lax.broadcasted_iota(jnp.int32, (BAND, DEG), 1)
    for s, (in_ref, out_ref) in enumerate(zip(ins, outs)):
        first = scalars_ref[LAT] + (scalars_ref[places[s]] + pl.program_id(0)) * count
        out_ref[...] = jnp.zeros(out_ref.shape, out_ref.dtype)
        for j in range(count):
            part = in_ref[j].astype(jnp.float32)
            part = jnp.where(degree >= first + j, part, 0.0)
            out_ref[j, :BAND, :DEG] = part.astype(out_ref.dtype)


def pass_kernel(in_ref, out_ref):
    for i in range(in_ref.shape[0]):
        out_ref[i] = in_ref[i]


def bring_kernel(table_hbm, table_ref, sem):
    copy = pltpu.make_async_copy(table_hbm, table_ref, sem)
    copy.start()
    copy.wait()


def part_of(p):
    return pl.ds(pl.multiple_of(p * PART, 8), PART)


def dft_kernel(quad_ref, x_ref, t_ref, out_ref, s_ref):
    step = pl.program_id(0)
    x = jnp.concatenate(
        [x_ref[:, 0].reshape(LON * PAD, CH), x_ref[:, 1].reshape(LON * PAD, CH)], axis=1
    )
    rows = 768

    @pl.loop(0, RM * ALL // rows)
    def _(chunk):
        t = t_ref[pl.ds(pl.multiple_of(chunk * rows, rows), rows), :]
        y = jnp.dot(t, x, preferred_element_type=jnp.float32)
        for j in range(2):
            a = 2 * step + j
            scaled = y[:, j * CH : (j + 1) * CH] * quad_ref[a]
            for k in range(rows // ALL):
                s_ref[pl.ds(a * RM + chunk * (rows // ALL) + k, ALL, stride=BLOCK), :] = scaled[
                    k * ALL : (k + 1) * ALL
                ]

    @pl.when(step == pl.num_programs(0) - 1)
    def _():
        widen(s_ref, out_ref, SPEC)


def legendre_kernel(src_ref, dest_ref, w_ref, *refs):
    legs, outs, (s_in, s_out) = refs[:LAT], refs[LAT:-2], refs[-2:]
    m = pl.program_id(0)

    @pl.when(m == 0)
    def _():
        widen(w_ref, s_in, SPEC)

    parts = []
    for s in range(LAT):
        base = src_ref[s] * (PAD * RM) + m
        parts.append(
            jnp.concatenate(
                [s_in[pl.ds(base + r * OWN, PAD, stride=RM), :] for r in range(2)], axis=1
            ).astype(jnp.bfloat16)
        )
    w = jnp.concatenate(parts, axis=0)
    leg = jnp.concatenate([leg_ref[0] for leg_ref in legs], axis=0)
    y = lax.dot_general(leg, w, (((0,), (0,)), ((), ())), preferred_element_type=jnp.float32)
    for r in range(2):
        s_out[pl.ds(r * OWN + m, DEG, stride=RM), :] = y[:DEG, r * CH : (r + 1) * CH]

    @pl.when(m == pl.num_programs(0) - 1)
    def _():
        for s, out_ref in enumerate(outs):
            out_ref[...] = s_out[part_of(dest_ref[s]), :].astype(out_ref.dtype)


def mix_kernel(*refs):
    n = (len(refs) - 4) // 2
    xs, (wr_ref, wi_ref), outs = refs[:n], refs[n : n + 2], refs[n + 2 : -2]
    s_in, s_out = refs[-2:]
    step = pl.program_id(0)

    @pl.when(step == 0)
    def _():
        for s, x_ref in enumerate(xs):
            s_in[part_of(s), :] = x_ref[...].astype(s_in.dtype)

    count = wr_ref.shape[0]
    for d in range(count):
        base = (step * count + d) * RM
        x = jnp.concatenate(
            [
                jnp.concatenate(
                    [s_in[pl.ds(base + r * OWN + j, n, stride=PART), :] for j in range(OWN)],
                    axis=0,
                )
                for r in range(2)
            ],
            axis=1,
        ).astype(jnp.bfloat16)
        wr, wi = wr_ref[d], wi_ref[d]
        w = jnp.concatenate(
            [jnp.concatenate([wr, wi], axis=1), jnp.concatenate([-wi, wr], axis=1)], axis=0
        )
        y = jnp.dot(x, w, preferred_element_type=jnp.float32)
        for r in range(2):
            for j in range(OWN):
                s_out[pl.ds(base + r * OWN + j, n, stride=PART), :] = y[
                    j * n : (j + 1) * n, r * CH : (r + 1) * CH
                ]

    @pl.when(step == pl.num_programs(0) - 1)
    def _():
        for s, out_ref in enumerate(outs):
            out_ref[...] = s_out[part_of(s), :].astype(out_ref.dtype)


def inverse_legendre_kernel(src_ref, dest_ref, *refs):
    xs, legs, (out_ref, s_in, s_out) = refs[:LAT], refs[LAT:-3], refs[-3:]
    m = pl.program_id(0)

    @pl.when(m == 0)
    def _():
        for s, x_ref in enumerate(xs):
            s_in[part_of(dest_ref[s]), :] = x_ref[...].astype(s_in.dtype)

    x = jnp.concatenate(
        [s_in[pl.ds(r * OWN + m, DEG, stride=RM), :] for r in range(2)], axis=1
    ).astype(jnp.bfloat16)
    x = jnp.concatenate([x, jnp.zeros((DEGPAD - DEG, 2 * CH), jnp.bfloat16)], axis=0)
    leg = jnp.concatenate([leg_ref[0] for leg_ref in legs], axis=0)
    y = jnp.dot(leg, x, preferred_element_type=jnp.float32)
    for s in range(LAT):
        base = src_ref[s] * (PAD * RM) + m
        for r in range(2):
            s_out[pl.ds(base + r * OWN, PAD, stride=RM), :] = y[
                s * PAD : (s + 1) * PAD, r * CH : (r + 1) * CH
            ]

    @pl.when(m == pl.num_programs(0) - 1)
    def _():
        widen(s_out, out_ref, SPEC)


def inverse_dft_kernel(x_ref, t_ref, out_ref, s_in):
    step = pl.program_id(0)

    @pl.when(step == 0)
    def _():
        widen(x_ref, s_in, SPEC)

    x = jnp.concatenate(
        [
            jnp.concatenate(
                [s_in[pl.ds((2 * step + j) * RM + k, ALL, stride=BLOCK), :] for k in range(RM)],
                axis=0,
            )
            for j in range(2)
        ],
        axis=1,
    ).astype(jnp.bfloat16)
    blocks = 8
    rows = blocks * PAD

    @pl.loop(0, LON // blocks)
    def _(chunk):
        t = t_ref[pl.ds(pl.multiple_of(chunk * rows, rows), rows), :]
        y = jnp.dot(t, x, preferred_element_type=jnp.float32).astype(jnp.bfloat16)
        for j in range(2):
            out_ref[pl.ds(chunk * blocks, blocks), j] = y[:, j * CH : (j + 1) * CH].reshape(
                blocks, PAD, CH
            )


def params(limit=VMEM):
    return pltpu.CompilerParams(dimension_semantics=("arbitrary",), vmem_limit_bytes=limit)


def whole(shape):
    return pl.BlockSpec(shape, lambda *_: (0,) * len(shape))


def cut(table, scalars, places):
    count, n = 3, len(places)
    return pl.pallas_call(
        functools.partial(cut_kernel, places),
        grid_spec=pltpu.PrefetchScalarGridSpec(
            num_scalar_prefetch=1,
            grid=(OWN // count,),
            in_specs=[
                pl.BlockSpec((count, BAND, DEG), lambda i, ref, s=s: (ref[s] + i, 0, 0))
                for s in places
            ],
            out_specs=[pl.BlockSpec((count, PAD, DEGPAD), lambda i, ref: (i, 0, 0))] * n,
        ),
        out_shape=[jax.ShapeDtypeStruct((OWN, PAD, DEGPAD), jnp.bfloat16)] * n,
        compiler_params=params(CUT_VMEM),
        cost_estimate=pl.CostEstimate(
            flops=1_000_000 * n, bytes_accessed=1_700_000 * n, transcendentals=0
        ),
        name="cut",
    )(scalars, *[table] * n)


ORDER = pl.CostEstimate(flops=60_000_000_000, bytes_accessed=200_000_000, transcendentals=0)


def in_order(token):
    return pl.pallas_call(
        pass_kernel,
        in_specs=[pl.BlockSpec(memory_space=pltpu.SMEM)],
        out_specs=pl.BlockSpec(memory_space=pltpu.SMEM),
        out_shape=jax.ShapeDtypeStruct(token.shape, token.dtype),
        compiler_params=pltpu.CompilerParams(vmem_limit_bytes=1024 * 1024),
        cost_estimate=ORDER,
        name="in_order",
    )(token)


def bring(table):
    return pl.pallas_call(
        bring_kernel,
        in_specs=[pl.BlockSpec(memory_space=pl.ANY)],
        out_specs=pl.BlockSpec(memory_space=pltpu.VMEM),
        out_shape=jax.ShapeDtypeStruct(table.shape, table.dtype),
        scratch_shapes=[pltpu.SemaphoreType.DMA],
        compiler_params=pltpu.CompilerParams(vmem_limit_bytes=12 * 1024 * 1024),
        name="bring",
    )(table)


def dft(quad, x, table):
    return pl.pallas_call(
        dft_kernel,
        grid=(OWN // 2,),
        in_specs=[
            pl.BlockSpec(memory_space=pltpu.SMEM),
            pl.BlockSpec((LON, 2, PAD, CH), lambda s: (0, s, 0, 0)),
            whole((RM * ALL, LON * PAD)),
        ],
        out_specs=whole((SPEC, CH)),
        out_shape=jax.ShapeDtypeStruct((SPEC, CH), jnp.bfloat16),
        scratch_shapes=[pltpu.VMEM((SPEC, CH), jnp.float32)],
        compiler_params=params(),
        cost_estimate=pl.CostEstimate(
            flops=1_000_000, bytes_accessed=100_000, transcendentals=0
        ),
        name="dft",
    )(quad, x, table)


def legendre_call(kernel, name, src, dest, xs, legs, rows_out, limit):
    rows_in = [x.shape[0] for x in xs]
    return pl.pallas_call(
        kernel,
        grid=(OWN,),
        in_specs=[pl.BlockSpec(memory_space=pltpu.SMEM)] * 2
        + [whole((rows, CH)) for rows in rows_in]
        + [pl.BlockSpec((1, PAD, DEGPAD), lambda m: (m, 0, 0))] * LAT,
        out_specs=[whole((rows, CH)) for rows in rows_out],
        out_shape=[jax.ShapeDtypeStruct((rows, CH), jnp.bfloat16) for rows in rows_out],
        scratch_shapes=[
            pltpu.VMEM((sum(rows_in), CH), jnp.float32),
            pltpu.VMEM((sum(rows_out), CH), jnp.float32),
        ],
        compiler_params=params(limit),
        cost_estimate=pl.CostEstimate(
            flops=2 * 6 * 768 * 768 * 256, bytes_accessed=12_000_000, transcendentals=0
        ),
        name=name,
    )(src, dest, *xs, *legs)


def mix(xs, wr, wi):
    n = len(xs)
    weight = pl.BlockSpec((STEP, CH, CH), lambda s: (s, 0, 0))
    return pl.pallas_call(
        mix_kernel,
        grid=(BAND // STEP,),
        in_specs=[whole((PART, CH))] * n + [weight, weight],
        out_specs=[whole((PART, CH))] * n,
        out_shape=[jax.ShapeDtypeStruct((PART, CH), jnp.bfloat16)] * n,
        scratch_shapes=[pltpu.VMEM((n * PART, CH), jnp.float32)] * 2,
        compiler_params=params(),
        cost_estimate=pl.CostEstimate(
            flops=2 * 90 * 48 * 256 * 256, bytes_accessed=10_000_000, transcendentals=0
        ),
        name="mix",
    )(*xs, wr, wi)


def inverse_dft(x, table):
    return pl.pallas_call(
        inverse_dft_kernel,
        grid=(OWN // 2,),
        in_specs=[whole((SPEC, CH)), whole((LON * PAD, RM * ALL))],
        out_specs=pl.BlockSpec((LON, 2, PAD, CH), lambda s: (0, s, 0, 0)),
        out_shape=jax.ShapeDtypeStruct((LON, OWN, PAD, CH), jnp.bfloat16),
        scratch_shapes=[pltpu.VMEM((SPEC, CH), jnp.float32)],
        compiler_params=params(),
        cost_estimate=pl.CostEstimate(
            flops=2 * 1536 * 1536 * 768, bytes_accessed=10_000_000, transcendentals=0
        ),
        name="inverse_dft",
    )(x, table)


def swap(x, axes):
    return lax.all_to_all(x, axes, split_axis=0, concat_axis=0, tiled=True)


def shifted(part, shift):
    if shift == 0:
        return part
    return lax.ppermute(part, "lat", [(i, (i + shift) % LAT) for i in range(LAT)])


def per_device(field, legendre, quadrature, mix_real, mix_imag):
    p = lax.axis_index("lat")
    q = lax.axis_index("lon")
    forward_table, inverse_table = make_tables()

    rows = swap(jnp.pad(field, ((0, PAD - BAND), (0, PAD - BAND), (0, 0))), "lon")

    orders = legendre.shape[0]
    table = jnp.transpose(legendre, (0, 2, 1))
    shifts = jnp.array(SHIFTS, jnp.int32)
    src = lax.rem(p - shifts + LAT, LAT)
    dest = lax.rem(p + jnp.array(SENDS, jnp.int32), LAT)
    cuts = [None] * LAT
    firsts = lax.rem(p + jnp.array(SHIFTS + (0,), jnp.int32), LAT) * (OWN // 3)
    firsts = jnp.minimum(firsts, (orders - OWN) // 3)
    scalars = jnp.where(jnp.arange(LAT + 1) == LAT, q * orders, firsts)
    for group in ((1, 2, 3, 4), (7,), (5, 6, 0)):
        parts = cut(table, scalars, group)
        table, *parts = lax.optimization_barrier((table, *parts))
        for i, part in zip(group, parts):
            cuts[i] = part
    quad = lax.dynamic_slice_in_dim(jnp.pad(quadrature, (0, PAD - BAND)), q * OWN, OWN, 0)

    legs = list(cuts)

    def end(value, places):
        parts = [shifted(cuts[i], SHIFTS[i]) for i in places]
        value, parts = lax.optimization_barrier((value, parts))
        for i, part in zip(places, parts):
            legs[i] = part
        return value

    dest = end(dest, (1, 2, 3, 4, 7))
    dest, forward_table = lax.optimization_barrier((dest, bring(jnp.asarray(forward_table))))
    dest = in_order(dest)
    cuts[5:7], rows, dest = lax.optimization_barrier((cuts[5:7], rows, dest))
    spectrum = dft(quad, rows.reshape(LON, OWN, PAD, CH), forward_table)
    dest = in_order(end(dest, (5, 6)))
    weighted = swap(spectrum, ("lat", "lon"))
    coefficients = legendre_call(
        legendre_kernel, "legendre", src, dest, [weighted], legs, [PART] * LAT, VMEM
    )
    mixed = []
    for group in GROUPS:
        parts = [shifted(coefficients[len(mixed) + i], shift) for i, shift in enumerate(group)]
        parts = mix(parts, mix_real, mix_imag)
        mixed += [shifted(part, (LAT - shift) % LAT) for part, shift in zip(parts, group)]
    (grid_spectrum,) = legendre_call(
        inverse_legendre_kernel, "inverse_legendre", src, dest, mixed, legs, [SPEC], VMEM
    )
    grid_spectrum = swap(grid_spectrum, ("lat", "lon"))
    samples = inverse_dft(grid_spectrum, jnp.asarray(inverse_table))
    synthesis = swap(samples.reshape(LON * OWN, PAD, CH), "lon")[:BAND, :BAND]
    return (field.astype(jnp.float32) + synthesis.astype(jnp.float32)).astype(jnp.bfloat16)


def solution(mesh):
    placed = (
        P("lat", "lon", None),
        P("lon", None, "lat"),
        P("lat"),
        P("lat", None, None),
        P("lat", None, None),
    )
    return jax.shard_map(
        per_device, mesh=mesh, in_specs=placed, out_specs=P("lat", "lon", None), check_vma=False
    )
```

```python
import jax
import jax.numpy as jnp
import ml_dtypes
import numpy as np
from jax import lax
from jax.experimental import pallas as pl
from jax.experimental.pallas import tpu as pltpu
from jax.sharding import PartitionSpec as P

LAT = 8
LON = 16
ALL = LAT * LON
BAND = 90
PAD = 96
OWN = 6
RM = 2 * OWN
BLOCK = OWN * RM
SPEC = ALL * BLOCK
DEG = 720
DEGPAD = 768
COEF = DEG * RM
PART = BAND * RM
STEP = 15
SHIFTS = (0, 1, 7, 2, 6, 3, 5, 4)
GROUPS = ((4, 3, 5), (2, 6, 1, 7, 0))
SENDS = GROUPS[0] + GROUPS[1]
CH = 128
FULL = 1440
VMEM = 24 * 1024 * 1024
CUT_VMEM = 58 * 1024 * 1024


def order_of():
    p = np.arange(LAT)[None, :, None]
    q = np.arange(LON)[None, None, :]
    j = np.arange(OWN)[:, None, None]
    first = np.minimum(6 * p, 45 - OWN)
    order = 45 * q + first + j
    valid = np.broadcast_to(first + j >= 6 * p, order.shape)
    return order.reshape(-1), valid.reshape(-1)


def make_tables():
    order, valid = order_of()
    n = np.arange(FULL)
    phase = (n[:, None] * order[None, :] % FULL).astype(np.float32) * np.float32(2.0 * np.pi / FULL)
    cosine = np.cos(phase.astype(np.float64)).astype(np.float32)
    sine = np.sin(phase.astype(np.float64)).astype(np.float32)
    both = np.concatenate([cosine, -sine], 1) * np.concatenate([valid, valid])[None, :]
    both = both.reshape(LON, BAND, 2 * OWN * ALL)
    both = np.pad(both, ((0, 0), (0, PAD - BAND), (0, 0))).reshape(LON * PAD, RM * ALL)
    forward = both * np.float32(1.0 / np.sqrt(np.float32(FULL)))
    inverse = both * np.sqrt(np.float32(2.0 / FULL))
    return (
        np.ascontiguousarray(forward.T).astype(ml_dtypes.bfloat16),
        np.ascontiguousarray(inverse).astype(ml_dtypes.bfloat16),
    )


def widen(src, dst, rows):
    step = 576

    @pl.loop(0, rows // step)
    def _(i):
        part = pl.ds(pl.multiple_of(i * step, step), step)
        dst[part, :] = src[part, :].astype(dst.dtype)


def cut_kernel(scalars_ref, *refs):
    ins, outs = refs[: len(refs) // 2], refs[len(refs) // 2 :]
    count = ins[0].shape[0]
    degree = lax.broadcasted_iota(jnp.int32, (BAND, DEG), 1)
    for s, (in_ref, out_ref) in enumerate(zip(ins, outs)):
        first = scalars_ref[len(ins)] + (scalars_ref[s] + pl.program_id(0)) * count
        out_ref[...] = jnp.zeros(out_ref.shape, out_ref.dtype)
        for j in range(count):
            part = in_ref[j].astype(jnp.float32)
            part = jnp.where(degree >= first + j, part, 0.0)
            out_ref[j, :BAND, :DEG] = part.astype(out_ref.dtype)


def pass_kernel(in_ref, out_ref):
    for i in range(in_ref.shape[0]):
        out_ref[i] = in_ref[i]


def part_of(p):
    return pl.ds(pl.multiple_of(p * PART, 8), PART)


def dft_kernel(quad_ref, x_ref, t_ref, out_ref, s_ref):
    step = pl.program_id(0)
    x = jnp.concatenate(
        [x_ref[:, 0].reshape(LON * PAD, CH), x_ref[:, 1].reshape(LON * PAD, CH)], axis=1
    )
    rows = 768

    @pl.loop(0, RM * ALL // rows)
    def _(chunk):
        t = t_ref[pl.ds(pl.multiple_of(chunk * rows, rows), rows), :]
        y = jnp.dot(t, x, preferred_element_type=jnp.float32)
        for j in range(2):
            a = 2 * step + j
            scaled = y[:, j * CH : (j + 1) * CH] * quad_ref[a]
            for k in range(rows // ALL):
                s_ref[pl.ds(a * RM + chunk * (rows // ALL) + k, ALL, stride=BLOCK), :] = scaled[
                    k * ALL : (k + 1) * ALL
                ]

    @pl.when(step == pl.num_programs(0) - 1)
    def _():
        widen(s_ref, out_ref, SPEC)


def legendre_kernel(src_ref, dest_ref, w_ref, *refs):
    legs, outs, (s_in, s_out) = refs[:LAT], refs[LAT:-2], refs[-2:]
    m = pl.program_id(0)

    @pl.when(m == 0)
    def _():
        widen(w_ref, s_in, SPEC)

    parts = []
    for s in range(LAT):
        base = src_ref[s] * (PAD * RM) + m
        parts.append(
            jnp.concatenate(
                [s_in[pl.ds(base + r * OWN, PAD, stride=RM), :] for r in range(2)], axis=1
            ).astype(jnp.bfloat16)
        )
    w = jnp.concatenate(parts, axis=0)
    leg = jnp.concatenate([leg_ref[0] for leg_ref in legs], axis=0)
    y = lax.dot_general(leg, w, (((0,), (0,)), ((), ())), preferred_element_type=jnp.float32)
    for r in range(2):
        s_out[pl.ds(r * OWN + m, DEG, stride=RM), :] = y[:DEG, r * CH : (r + 1) * CH]

    @pl.when(m == pl.num_programs(0) - 1)
    def _():
        for s, out_ref in enumerate(outs):
            out_ref[...] = s_out[part_of(dest_ref[s]), :].astype(out_ref.dtype)


def mix_kernel(*refs):
    n = (len(refs) - 4) // 2
    xs, (wr_ref, wi_ref), outs = refs[:n], refs[n : n + 2], refs[n + 2 : -2]
    s_in, s_out = refs[-2:]
    step = pl.program_id(0)

    @pl.when(step == 0)
    def _():
        for s, x_ref in enumerate(xs):
            s_in[part_of(s), :] = x_ref[...].astype(s_in.dtype)

    count = wr_ref.shape[0]
    for d in range(count):
        base = (step * count + d) * RM
        x = jnp.concatenate(
            [
                jnp.concatenate(
                    [s_in[pl.ds(base + r * OWN + j, n, stride=PART), :] for j in range(OWN)],
                    axis=0,
                )
                for r in range(2)
            ],
            axis=1,
        ).astype(jnp.bfloat16)
        wr, wi = wr_ref[d], wi_ref[d]
        w = jnp.concatenate(
            [jnp.concatenate([wr, wi], axis=1), jnp.concatenate([-wi, wr], axis=1)], axis=0
        )
        y = jnp.dot(x, w, preferred_element_type=jnp.float32)
        for r in range(2):
            for j in range(OWN):
                s_out[pl.ds(base + r * OWN + j, n, stride=PART), :] = y[
                    j * n : (j + 1) * n, r * CH : (r + 1) * CH
                ]

    @pl.when(step == pl.num_programs(0) - 1)
    def _():
        for s, out_ref in enumerate(outs):
            out_ref[...] = s_out[part_of(s), :].astype(out_ref.dtype)


def inverse_legendre_kernel(src_ref, dest_ref, *refs):
    xs, legs, (out_ref, s_in, s_out) = refs[:LAT], refs[LAT:-3], refs[-3:]
    m = pl.program_id(0)

    @pl.when(m == 0)
    def _():
        for s, x_ref in enumerate(xs):
            s_in[part_of(dest_ref[s]), :] = x_ref[...].astype(s_in.dtype)

    x = jnp.concatenate(
        [s_in[pl.ds(r * OWN + m, DEG, stride=RM), :] for r in range(2)], axis=1
    ).astype(jnp.bfloat16)
    x = jnp.concatenate([x, jnp.zeros((DEGPAD - DEG, 2 * CH), jnp.bfloat16)], axis=0)
    leg = jnp.concatenate([leg_ref[0] for leg_ref in legs], axis=0)
    y = jnp.dot(leg, x, preferred_element_type=jnp.float32)
    for s in range(LAT):
        base = src_ref[s] * (PAD * RM) + m
        for r in range(2):
            s_out[pl.ds(base + r * OWN, PAD, stride=RM), :] = y[
                s * PAD : (s + 1) * PAD, r * CH : (r + 1) * CH
            ]

    @pl.when(m == pl.num_programs(0) - 1)
    def _():
        widen(s_out, out_ref, SPEC)


def inverse_dft_kernel(x_ref, t_ref, out_ref, s_in):
    step = pl.program_id(0)

    @pl.when(step == 0)
    def _():
        widen(x_ref, s_in, SPEC)

    x = jnp.concatenate(
        [
            jnp.concatenate(
                [s_in[pl.ds((2 * step + j) * RM + k, ALL, stride=BLOCK), :] for k in range(RM)],
                axis=0,
            )
            for j in range(2)
        ],
        axis=1,
    ).astype(jnp.bfloat16)
    blocks = 8
    rows = blocks * PAD

    @pl.loop(0, LON // blocks)
    def _(chunk):
        t = t_ref[pl.ds(pl.multiple_of(chunk * rows, rows), rows), :]
        y = jnp.dot(t, x, preferred_element_type=jnp.float32).astype(jnp.bfloat16)
        for j in range(2):
            out_ref[pl.ds(chunk * blocks, blocks), j] = y[:, j * CH : (j + 1) * CH].reshape(
                blocks, PAD, CH
            )


def params(limit=VMEM):
    return pltpu.CompilerParams(dimension_semantics=("arbitrary",), vmem_limit_bytes=limit)


def whole(shape):
    return pl.BlockSpec(shape, lambda *_: (0,) * len(shape))


def cut(table, scalars, n):
    count = 3
    return pl.pallas_call(
        cut_kernel,
        grid_spec=pltpu.PrefetchScalarGridSpec(
            num_scalar_prefetch=1,
            grid=(OWN // count,),
            in_specs=[
                pl.BlockSpec((count, BAND, DEG), lambda i, ref, s=s: (ref[s] + i, 0, 0))
                for s in range(n)
            ],
            out_specs=[pl.BlockSpec((count, PAD, DEGPAD), lambda i, ref: (i, 0, 0))] * n,
        ),
        out_shape=[jax.ShapeDtypeStruct((OWN, PAD, DEGPAD), jnp.bfloat16)] * n,
        compiler_params=params(CUT_VMEM),
        cost_estimate=pl.CostEstimate(
            flops=1_000_000 * n, bytes_accessed=1_700_000 * n, transcendentals=0
        ),
        name="cut",
    )(scalars, *[table] * n)


def in_order(token):
    return pl.pallas_call(
        pass_kernel,
        in_specs=[pl.BlockSpec(memory_space=pltpu.SMEM)],
        out_specs=pl.BlockSpec(memory_space=pltpu.SMEM),
        out_shape=jax.ShapeDtypeStruct(token.shape, token.dtype),
        compiler_params=pltpu.CompilerParams(vmem_limit_bytes=1024 * 1024),
        cost_estimate=pl.CostEstimate(
            flops=60_000_000_000, bytes_accessed=200_000_000, transcendentals=0
        ),
        name="in_order",
    )(token)


def dft(quad, x, table):
    return pl.pallas_call(
        dft_kernel,
        grid=(OWN // 2,),
        in_specs=[
            pl.BlockSpec(memory_space=pltpu.SMEM),
            pl.BlockSpec((LON, 2, PAD, CH), lambda s: (0, s, 0, 0)),
            whole((RM * ALL, LON * PAD)),
        ],
        out_specs=whole((SPEC, CH)),
        out_shape=jax.ShapeDtypeStruct((SPEC, CH), jnp.bfloat16),
        scratch_shapes=[pltpu.VMEM((SPEC, CH), jnp.float32)],
        compiler_params=params(),
        cost_estimate=pl.CostEstimate(
            flops=1_000_000, bytes_accessed=100_000, transcendentals=0
        ),
        name="dft",
    )(quad, x, table)


def legendre_call(kernel, name, src, dest, xs, legs, rows_out, limit):
    rows_in = [x.shape[0] for x in xs]
    return pl.pallas_call(
        kernel,
        grid=(OWN,),
        in_specs=[pl.BlockSpec(memory_space=pltpu.SMEM)] * 2
        + [whole((rows, CH)) for rows in rows_in]
        + [pl.BlockSpec((1, PAD, DEGPAD), lambda m: (m, 0, 0))] * LAT,
        out_specs=[whole((rows, CH)) for rows in rows_out],
        out_shape=[jax.ShapeDtypeStruct((rows, CH), jnp.bfloat16) for rows in rows_out],
        scratch_shapes=[
            pltpu.VMEM((sum(rows_in), CH), jnp.float32),
            pltpu.VMEM((sum(rows_out), CH), jnp.float32),
        ],
        compiler_params=params(limit),
        cost_estimate=pl.CostEstimate(
            flops=2 * 6 * 768 * 768 * 256, bytes_accessed=12_000_000, transcendentals=0
        ),
        name=name,
    )(src, dest, *xs, *legs)


def mix(xs, wr, wi):
    n = len(xs)
    weight = pl.BlockSpec((STEP, CH, CH), lambda s: (s, 0, 0))
    return pl.pallas_call(
        mix_kernel,
        grid=(BAND // STEP,),
        in_specs=[whole((PART, CH))] * n + [weight, weight],
        out_specs=[whole((PART, CH))] * n,
        out_shape=[jax.ShapeDtypeStruct((PART, CH), jnp.bfloat16)] * n,
        scratch_shapes=[pltpu.VMEM((n * PART, CH), jnp.float32)] * 2,
        compiler_params=params(),
        cost_estimate=pl.CostEstimate(
            flops=2 * 90 * 48 * 256 * 256, bytes_accessed=10_000_000, transcendentals=0
        ),
        name="mix",
    )(*xs, wr, wi)


def inverse_dft(x, table):
    return pl.pallas_call(
        inverse_dft_kernel,
        grid=(OWN // 2,),
        in_specs=[whole((SPEC, CH)), whole((LON * PAD, RM * ALL))],
        out_specs=pl.BlockSpec((LON, 2, PAD, CH), lambda s: (0, s, 0, 0)),
        out_shape=jax.ShapeDtypeStruct((LON, OWN, PAD, CH), jnp.bfloat16),
        scratch_shapes=[pltpu.VMEM((SPEC, CH), jnp.float32)],
        compiler_params=params(),
        cost_estimate=pl.CostEstimate(
            flops=2 * 1536 * 1536 * 768, bytes_accessed=10_000_000, transcendentals=0
        ),
        name="inverse_dft",
    )(x, table)


def swap(x, axes):
    return lax.all_to_all(x, axes, split_axis=0, concat_axis=0, tiled=True)


def shifted(part, shift):
    if shift == 0:
        return part
    return lax.ppermute(part, "lat", [(i, (i + shift) % LAT) for i in range(LAT)])


def per_device(field, legendre, quadrature, mix_real, mix_imag):
    p = lax.axis_index("lat")
    q = lax.axis_index("lon")
    forward_table, inverse_table = make_tables()

    rows = swap(jnp.pad(field, ((0, PAD - BAND), (0, PAD - BAND), (0, 0))), "lon")

    orders = legendre.shape[0]
    table = jnp.transpose(legendre, (0, 2, 1))
    shifts = jnp.array(SHIFTS, jnp.int32)
    src = lax.rem(p - shifts + LAT, LAT)
    dest = lax.rem(p + jnp.array(SENDS, jnp.int32), LAT)
    cuts = [None] * LAT
    for group in ((1, 2, 3, 4), (5, 6, 7, 0)):
        moves = jnp.array([SHIFTS[i] for i in group] + [0], jnp.int32)
        firsts = jnp.minimum(lax.rem(p + moves, LAT) * (OWN // 3), (orders - OWN) // 3)
        scalars = jnp.where(jnp.arange(len(group) + 1) == len(group), q * orders, firsts)
        parts = cut(table, scalars, len(group))
        table, *parts = lax.optimization_barrier((table, *parts))
        for i, part in zip(group, parts):
            cuts[i] = part
    quad = lax.dynamic_slice_in_dim(jnp.pad(quadrature, (0, PAD - BAND)), q * OWN, OWN, 0)

    legs = list(cuts)

    def end(value, places):
        parts = [shifted(cuts[i], SHIFTS[i]) for i in places]
        value, parts = lax.optimization_barrier((value, parts))
        for i, part in zip(places, parts):
            legs[i] = part
        return value

    dest = in_order(end(dest, (1, 2, 3, 4, 7)))
    cuts[5:7], dest = lax.optimization_barrier((cuts[5:7], dest))
    rows, dest = lax.optimization_barrier((rows, dest))
    spectrum = dft(quad, rows.reshape(LON, OWN, PAD, CH), jnp.asarray(forward_table))
    dest = in_order(end(dest, (5, 6)))
    weighted = swap(spectrum, ("lat", "lon"))
    coefficients = legendre_call(
        legendre_kernel, "legendre", src, dest, [weighted], legs, [PART] * LAT, VMEM
    )
    mixed = []
    for group in GROUPS:
        parts = [shifted(coefficients[len(mixed) + i], shift) for i, shift in enumerate(group)]
        parts = mix(parts, mix_real, mix_imag)
        mixed += [shifted(part, (LAT - shift) % LAT) for part, shift in zip(parts, group)]
    (grid_spectrum,) = legendre_call(
        inverse_legendre_kernel, "inverse_legendre", src, dest, mixed, legs, [SPEC], VMEM
    )
    grid_spectrum = swap(grid_spectrum, ("lat", "lon"))
    samples = inverse_dft(grid_spectrum, jnp.asarray(inverse_table))
    synthesis = swap(samples.reshape(LON * OWN, PAD, CH), "lon")[:BAND, :BAND]
    return (field.astype(jnp.float32) + synthesis.astype(jnp.float32)).astype(jnp.bfloat16)


def solution(mesh):
    placed = (
        P("lat", "lon", None),
        P("lon", None, "lat"),
        P("lat"),
        P("lat", None, None),
        P("lat", None, None),
    )
    return jax.shard_map(
        per_device, mesh=mesh, in_specs=placed, out_specs=P("lat", "lon", None), check_vma=False
    )
```

```python
import functools

import jax
import jax.numpy as jnp
import ml_dtypes
import numpy as np
from jax import lax
from jax.experimental import pallas as pl
from jax.experimental.pallas import tpu as pltpu
from jax.sharding import PartitionSpec as P

LAT = 8
LON = 16
ALL = LAT * LON
BAND = 90
PAD = 96
OWN = 6
RM = 2 * OWN
BLOCK = OWN * RM
SPEC = ALL * BLOCK
DEG = 720
DEGPAD = 768
COEF = DEG * RM
PART = BAND * RM
STEP = 15
SHIFTS = (0, 1, 7, 2, 6, 3, 5, 4)
GROUPS = ((4, 3, 5), (2, 6, 1, 7, 0))
SENDS = GROUPS[0] + GROUPS[1]
CH = 128
FULL = 1440
VMEM = 24 * 1024 * 1024
CUT_VMEM = 58 * 1024 * 1024


def order_of():
    p = np.arange(LAT)[None, :, None]
    q = np.arange(LON)[None, None, :]
    j = np.arange(OWN)[:, None, None]
    first = np.minimum(6 * p, 45 - OWN)
    order = 45 * q + first + j
    valid = np.broadcast_to(first + j >= 6 * p, order.shape)
    return order.reshape(-1), valid.reshape(-1)


def make_tables():
    order, valid = order_of()
    n = np.arange(FULL)
    phase = (n[:, None] * order[None, :] % FULL).astype(np.float32) * np.float32(2.0 * np.pi / FULL)
    cosine = np.cos(phase.astype(np.float64)).astype(np.float32)
    sine = np.sin(phase.astype(np.float64)).astype(np.float32)
    both = np.concatenate([cosine, -sine], 1) * np.concatenate([valid, valid])[None, :]
    both = both.reshape(LON, BAND, 2 * OWN * ALL)
    both = np.pad(both, ((0, 0), (0, PAD - BAND), (0, 0))).reshape(LON * PAD, RM * ALL)
    forward = both * np.float32(1.0 / np.sqrt(np.float32(FULL)))
    inverse = both * np.sqrt(np.float32(2.0 / FULL))
    return (
        np.ascontiguousarray(forward.T).astype(ml_dtypes.bfloat16),
        np.ascontiguousarray(inverse).astype(ml_dtypes.bfloat16),
    )


def widen(src, dst, rows):
    step = 576

    @pl.loop(0, rows // step)
    def _(i):
        part = pl.ds(pl.multiple_of(i * step, step), step)
        dst[part, :] = src[part, :].astype(dst.dtype)


def block_of(p, s):
    return jnp.minimum(lax.rem(p + SHIFTS[s], LAT) * (OWN // 3), 45 // 3 - OWN // 3)


def cut_kernel(places, p_ref, q_ref, *refs):
    ins, outs = refs[: len(refs) // 2], refs[len(refs) // 2 :]
    count = ins[0].shape[0]
    degree = lax.broadcasted_iota(jnp.int32, (BAND, DEG), 1)
    for s, in_ref, out_ref in zip(places, ins, outs):
        first = q_ref[0] * 45 + (block_of(p_ref[0], s) + pl.program_id(0)) * count
        out_ref[:, PAD - 16 :, :] = jnp.zeros((count, 16, DEGPAD), out_ref.dtype)
        out_ref[:, :, DEGPAD - CH :] = jnp.zeros((count, PAD, CH), out_ref.dtype)
        for j in range(count):
            part = in_ref[j].astype(jnp.float32)
            part = jnp.where(degree >= first + j, part, 0.0)
            out_ref[j, :BAND, :DEG] = part.astype(out_ref.dtype)


def pass_kernel(in_ref, out_ref):
    for i in range(in_ref.shape[0]):
        out_ref[i] = in_ref[i]


def part_of(p):
    return pl.ds(pl.multiple_of(p * PART, 8), PART)


def dft_kernel(quad_ref, x_ref, t_ref, out_ref, s_ref):
    step = pl.program_id(0)
    x = jnp.concatenate(
        [x_ref[:, 0].reshape(LON * PAD, CH), x_ref[:, 1].reshape(LON * PAD, CH)], axis=1
    )
    rows = 768

    @pl.loop(0, RM * ALL // rows)
    def _(chunk):
        t = t_ref[pl.ds(pl.multiple_of(chunk * rows, rows), rows), :]
        y = jnp.dot(t, x, preferred_element_type=jnp.float32)
        for j in range(2):
            a = 2 * step + j
            scaled = y[:, j * CH : (j + 1) * CH] * quad_ref[a]
            for k in range(rows // ALL):
                s_ref[pl.ds(a * RM + chunk * (rows // ALL) + k, ALL, stride=BLOCK), :] = scaled[
                    k * ALL : (k + 1) * ALL
                ]

    @pl.when(step == pl.num_programs(0) - 1)
    def _():
        widen(s_ref, out_ref, SPEC)


def legendre_kernel(src_ref, dest_ref, w_ref, *refs):
    legs, outs, (s_in, s_out) = refs[:LAT], refs[LAT:-2], refs[-2:]
    m = pl.program_id(0)

    @pl.when(m == 0)
    def _():
        widen(w_ref, s_in, SPEC)

    parts = []
    for s in range(LAT):
        base = src_ref[s] * (PAD * RM) + m
        parts.append(
            jnp.concatenate(
                [s_in[pl.ds(base + r * OWN, PAD, stride=RM), :] for r in range(2)], axis=1
            ).astype(jnp.bfloat16)
        )
    w = jnp.concatenate(parts, axis=0)
    leg = jnp.concatenate([leg_ref[0] for leg_ref in legs], axis=0)
    y = lax.dot_general(leg, w, (((0,), (0,)), ((), ())), preferred_element_type=jnp.float32)
    for r in range(2):
        s_out[pl.ds(r * OWN + m, DEG, stride=RM), :] = y[:DEG, r * CH : (r + 1) * CH]

    @pl.when(m == pl.num_programs(0) - 1)
    def _():
        for s, out_ref in enumerate(outs):
            out_ref[...] = s_out[part_of(dest_ref[s]), :].astype(out_ref.dtype)


def mix_kernel(*refs):
    n = (len(refs) - 4) // 2
    xs, (wr_ref, wi_ref), outs = refs[:n], refs[n : n + 2], refs[n + 2 : -2]
    s_in, s_out = refs[-2:]
    step = pl.program_id(0)

    @pl.when(step == 0)
    def _():
        for s, x_ref in enumerate(xs):
            s_in[part_of(s), :] = x_ref[...].astype(s_in.dtype)

    count = wr_ref.shape[0]
    for d in range(count):
        base = (step * count + d) * RM
        x = jnp.concatenate(
            [
                jnp.concatenate(
                    [s_in[pl.ds(base + r * OWN + j, n, stride=PART), :] for j in range(OWN)],
                    axis=0,
                )
                for r in range(2)
            ],
            axis=1,
        ).astype(jnp.bfloat16)
        wr, wi = wr_ref[d], wi_ref[d]
        w = jnp.concatenate(
            [jnp.concatenate([wr, wi], axis=1), jnp.concatenate([-wi, wr], axis=1)], axis=0
        )
        y = jnp.dot(x, w, preferred_element_type=jnp.float32)
        for r in range(2):
            for j in range(OWN):
                s_out[pl.ds(base + r * OWN + j, n, stride=PART), :] = y[
                    j * n : (j + 1) * n, r * CH : (r + 1) * CH
                ]

    @pl.when(step == pl.num_programs(0) - 1)
    def _():
        for s, out_ref in enumerate(outs):
            out_ref[...] = s_out[part_of(s), :].astype(out_ref.dtype)


def inverse_legendre_kernel(src_ref, dest_ref, *refs):
    xs, legs, (out_ref, s_in, s_out) = refs[:LAT], refs[LAT:-3], refs[-3:]
    m = pl.program_id(0)

    @pl.when(m == 0)
    def _():
        for s, x_ref in enumerate(xs):
            s_in[part_of(dest_ref[s]), :] = x_ref[...].astype(s_in.dtype)

    x = jnp.concatenate(
        [s_in[pl.ds(r * OWN + m, DEG, stride=RM), :] for r in range(2)], axis=1
    ).astype(jnp.bfloat16)
    x = jnp.concatenate([x, jnp.zeros((DEGPAD - DEG, 2 * CH), jnp.bfloat16)], axis=0)
    leg = jnp.concatenate([leg_ref[0] for leg_ref in legs], axis=0)
    y = jnp.dot(leg, x, preferred_element_type=jnp.float32)
    for s in range(LAT):
        base = src_ref[s] * (PAD * RM) + m
        for r in range(2):
            s_out[pl.ds(base + r * OWN, PAD, stride=RM), :] = y[
                s * PAD : (s + 1) * PAD, r * CH : (r + 1) * CH
            ]

    @pl.when(m == pl.num_programs(0) - 1)
    def _():
        widen(s_out, out_ref, SPEC)


def inverse_dft_kernel(x_ref, t_ref, out_ref, s_in):
    step = pl.program_id(0)

    @pl.when(step == 0)
    def _():
        widen(x_ref, s_in, SPEC)

    x = jnp.concatenate(
        [
            jnp.concatenate(
                [s_in[pl.ds((2 * step + j) * RM + k, ALL, stride=BLOCK), :] for k in range(RM)],
                axis=0,
            )
            for j in range(2)
        ],
        axis=1,
    ).astype(jnp.bfloat16)
    blocks = 8
    rows = blocks * PAD

    @pl.loop(0, LON // blocks)
    def _(chunk):
        t = t_ref[pl.ds(pl.multiple_of(chunk * rows, rows), rows), :]
        y = jnp.dot(t, x, preferred_element_type=jnp.float32).astype(jnp.bfloat16)
        for j in range(2):
            out_ref[pl.ds(chunk * blocks, blocks), j] = y[:, j * CH : (j + 1) * CH].reshape(
                blocks, PAD, CH
            )


def params(limit=VMEM):
    return pltpu.CompilerParams(dimension_semantics=("arbitrary",), vmem_limit_bytes=limit)


def whole(shape):
    return pl.BlockSpec(shape, lambda *_: (0,) * len(shape))


def cut(table, p, q, places):
    count, n = 3, len(places)
    return pl.pallas_call(
        functools.partial(cut_kernel, places),
        grid_spec=pltpu.PrefetchScalarGridSpec(
            num_scalar_prefetch=2,
            grid=(OWN // count,),
            in_specs=[
                pl.BlockSpec((count, BAND, DEG), lambda i, p, q, s=s: (block_of(p[0], s) + i, 0, 0))
                for s in places
            ],
            out_specs=[pl.BlockSpec((count, PAD, DEGPAD), lambda i, p, q: (i, 0, 0))] * n,
        ),
        out_shape=[jax.ShapeDtypeStruct((OWN, PAD, DEGPAD), jnp.bfloat16)] * n,
        compiler_params=params(CUT_VMEM),
        cost_estimate=pl.CostEstimate(
            flops=1_000_000 * n, bytes_accessed=1_700_000 * n, transcendentals=0
        ),
        name="cut",
    )(p.reshape(1), q.reshape(1), *[table] * n)


def in_order(token):
    return pl.pallas_call(
        pass_kernel,
        in_specs=[pl.BlockSpec(memory_space=pltpu.SMEM)],
        out_specs=pl.BlockSpec(memory_space=pltpu.SMEM),
        out_shape=jax.ShapeDtypeStruct(token.shape, token.dtype),
        compiler_params=pltpu.CompilerParams(vmem_limit_bytes=1024 * 1024),
        cost_estimate=pl.CostEstimate(
            flops=60_000_000_000, bytes_accessed=200_000_000, transcendentals=0
        ),
        name="in_order",
    )(token)


def dft(quad, x, table):
    return pl.pallas_call(
        dft_kernel,
        grid=(OWN // 2,),
        in_specs=[
            pl.BlockSpec(memory_space=pltpu.SMEM),
            pl.BlockSpec((LON, 2, PAD, CH), lambda s: (0, s, 0, 0)),
            whole((RM * ALL, LON * PAD)),
        ],
        out_specs=whole((SPEC, CH)),
        out_shape=jax.ShapeDtypeStruct((SPEC, CH), jnp.bfloat16),
        scratch_shapes=[pltpu.VMEM((SPEC, CH), jnp.float32)],
        compiler_params=params(),
        cost_estimate=pl.CostEstimate(
            flops=1_000_000, bytes_accessed=100_000, transcendentals=0
        ),
        name="dft",
    )(quad, x, table)


def legendre_call(kernel, name, src, dest, xs, legs, rows_out, limit):
    rows_in = [x.shape[0] for x in xs]
    return pl.pallas_call(
        kernel,
        grid=(OWN,),
        in_specs=[pl.BlockSpec(memory_space=pltpu.SMEM)] * 2
        + [whole((rows, CH)) for rows in rows_in]
        + [pl.BlockSpec((1, PAD, DEGPAD), lambda m: (m, 0, 0))] * LAT,
        out_specs=[whole((rows, CH)) for rows in rows_out],
        out_shape=[jax.ShapeDtypeStruct((rows, CH), jnp.bfloat16) for rows in rows_out],
        scratch_shapes=[
            pltpu.VMEM((sum(rows_in), CH), jnp.float32),
            pltpu.VMEM((sum(rows_out), CH), jnp.float32),
        ],
        compiler_params=params(limit),
        cost_estimate=pl.CostEstimate(
            flops=2 * 6 * 768 * 768 * 256, bytes_accessed=12_000_000, transcendentals=0
        ),
        name=name,
    )(src, dest, *xs, *legs)


def mix(xs, wr, wi):
    n = len(xs)
    weight = pl.BlockSpec((STEP, CH, CH), lambda s: (s, 0, 0))
    return pl.pallas_call(
        mix_kernel,
        grid=(BAND // STEP,),
        in_specs=[whole((PART, CH))] * n + [weight, weight],
        out_specs=[whole((PART, CH))] * n,
        out_shape=[jax.ShapeDtypeStruct((PART, CH), jnp.bfloat16)] * n,
        scratch_shapes=[pltpu.VMEM((n * PART, CH), jnp.float32)] * 2,
        compiler_params=params(),
        cost_estimate=pl.CostEstimate(
            flops=2 * 90 * 48 * 256 * 256, bytes_accessed=10_000_000, transcendentals=0
        ),
        name="mix",
    )(*xs, wr, wi)


def inverse_dft(x, table):
    return pl.pallas_call(
        inverse_dft_kernel,
        grid=(OWN // 2,),
        in_specs=[whole((SPEC, CH)), whole((LON * PAD, RM * ALL))],
        out_specs=pl.BlockSpec((LON, 2, PAD, CH), lambda s: (0, s, 0, 0)),
        out_shape=jax.ShapeDtypeStruct((LON, OWN, PAD, CH), jnp.bfloat16),
        scratch_shapes=[pltpu.VMEM((SPEC, CH), jnp.float32)],
        compiler_params=params(),
        cost_estimate=pl.CostEstimate(
            flops=2 * 1536 * 1536 * 768, bytes_accessed=10_000_000, transcendentals=0
        ),
        name="inverse_dft",
    )(x, table)


def swap(x, axes):
    return lax.all_to_all(x, axes, split_axis=0, concat_axis=0, tiled=True)


def shifted(part, shift):
    if shift == 0:
        return part
    return lax.ppermute(part, "lat", [(i, (i + shift) % LAT) for i in range(LAT)])


def per_device(field, legendre, quadrature, mix_real, mix_imag):
    p = lax.axis_index("lat")
    q = lax.axis_index("lon")
    forward_table, inverse_table = make_tables()

    rows = swap(jnp.pad(field, ((0, PAD - BAND), (0, PAD - BAND), (0, 0))), "lon")

    table = jnp.transpose(legendre, (0, 2, 1))
    shifts = jnp.array(SHIFTS, jnp.int32)
    src = lax.rem(p - shifts + LAT, LAT)
    dest = lax.rem(p + jnp.array(SENDS, jnp.int32), LAT)
    cuts = [None] * LAT
    for group in ((1, 2), (3, 4), (5, 6, 7, 0)):
        parts = cut(table, p, q, group)
        table, *parts = lax.optimization_barrier((table, *parts))
        for i, part in zip(group, parts):
            cuts[i] = part
    quad = lax.dynamic_slice_in_dim(jnp.pad(quadrature, (0, PAD - BAND)), q * OWN, OWN, 0)

    legs = list(cuts)

    def end(value, places):
        parts = [shifted(cuts[i], SHIFTS[i]) for i in places]
        value, parts = lax.optimization_barrier((value, parts))
        for i, part in zip(places, parts):
            legs[i] = part
        return value

    dest = in_order(end(dest, (1, 2, 3, 4, 7)))
    cuts[5:7], dest = lax.optimization_barrier((cuts[5:7], dest))
    rows, dest = lax.optimization_barrier((rows, dest))
    spectrum = dft(quad, rows.reshape(LON, OWN, PAD, CH), jnp.asarray(forward_table))
    dest = in_order(end(dest, (5, 6)))
    weighted = swap(spectrum, ("lat", "lon"))
    coefficients = legendre_call(
        legendre_kernel, "legendre", src, dest, [weighted], legs, [PART] * LAT, VMEM
    )
    mixed = []
    for group in GROUPS:
        parts = [shifted(coefficients[len(mixed) + i], shift) for i, shift in enumerate(group)]
        parts = mix(parts, mix_real, mix_imag)
        mixed += [shifted(part, (LAT - shift) % LAT) for part, shift in zip(parts, group)]
    (grid_spectrum,) = legendre_call(
        inverse_legendre_kernel, "inverse_legendre", src, dest, mixed, legs, [SPEC], VMEM
    )
    grid_spectrum = swap(grid_spectrum, ("lat", "lon"))
    samples = inverse_dft(grid_spectrum, jnp.asarray(inverse_table))
    synthesis = swap(samples.reshape(LON * OWN, PAD, CH), "lon")[:BAND, :BAND]
    return (field.astype(jnp.float32) + synthesis.astype(jnp.float32)).astype(jnp.bfloat16)


def solution(mesh):
    placed = (
        P("lat", "lon", None),
        P("lon", None, "lat"),
        P("lat"),
        P("lat", None, None),
        P("lat", None, None),
    )
    return jax.shard_map(
        per_device, mesh=mesh, in_specs=placed, out_specs=P("lat", "lon", None), check_vma=False
    )
```

```python
import functools

import jax
import jax.numpy as jnp
import ml_dtypes
import numpy as np
from jax import lax
from jax.experimental import pallas as pl
from jax.experimental.pallas import tpu as pltpu
from jax.sharding import PartitionSpec as P

LAT = 8
LON = 16
ALL = LAT * LON
BAND = 90
PAD = 96
OWN = 6
RM = 2 * OWN
BLOCK = OWN * RM
SPEC = ALL * BLOCK
DEG = 720
DEGPAD = 768
COEF = DEG * RM
PART = BAND * RM
STEP = 30
SHIFTS = (0, 1, 7, 2, 6, 3, 5, 4)
GROUPS = ((4, 3, 5), (2, 6, 1, 7, 0))
SENDS = GROUPS[0] + GROUPS[1]
CH = 128
FULL = 1440
VMEM = 24 * 1024 * 1024
CUT_VMEM = 58 * 1024 * 1024


def order_of():
    p = np.arange(LAT)[None, :, None]
    q = np.arange(LON)[None, None, :]
    j = np.arange(OWN)[:, None, None]
    first = np.minimum(6 * p, 45 - OWN)
    order = 45 * q + first + j
    valid = np.broadcast_to(first + j >= 6 * p, order.shape)
    return order.reshape(-1), valid.reshape(-1)


def make_tables():
    order, valid = order_of()
    n = np.arange(FULL)
    phase = (n[:, None] * order[None, :] % FULL).astype(np.float32) * np.float32(2.0 * np.pi / FULL)
    cosine = np.cos(phase.astype(np.float64)).astype(np.float32)
    sine = np.sin(phase.astype(np.float64)).astype(np.float32)
    both = np.concatenate([cosine, -sine], 1) * np.concatenate([valid, valid])[None, :]
    both = both.reshape(LON, BAND, 2 * OWN * ALL)
    both = np.pad(both, ((0, 0), (0, PAD - BAND), (0, 0))).reshape(LON * PAD, RM * ALL)
    forward = both * np.float32(1.0 / np.sqrt(np.float32(FULL)))
    inverse = both * np.sqrt(np.float32(2.0 / FULL))
    return (
        np.ascontiguousarray(forward.T).astype(ml_dtypes.bfloat16),
        np.ascontiguousarray(inverse).astype(ml_dtypes.bfloat16),
    )


def widen(src, dst, rows):
    step = 576

    @pl.loop(0, rows // step)
    def _(i):
        part = pl.ds(pl.multiple_of(i * step, step), step)
        dst[part, :] = src[part, :].astype(dst.dtype)


def block_of(p, s):
    return jnp.minimum(lax.rem(p + SHIFTS[s], LAT) * (OWN // 3), 45 // 3 - OWN // 3)


def cut_kernel(places, p_ref, q_ref, *refs):
    ins, outs = refs[: len(refs) // 2], refs[len(refs) // 2 :]
    count = ins[0].shape[0]
    degree = lax.broadcasted_iota(jnp.int32, (BAND, DEG), 1)
    for s, in_ref, out_ref in zip(places, ins, outs):
        first = q_ref[0] * 45 + (block_of(p_ref[0], s) + pl.program_id(0)) * count
        out_ref[:, PAD - 16 :, :] = jnp.zeros((count, 16, DEGPAD), out_ref.dtype)
        out_ref[:, :, DEGPAD - CH :] = jnp.zeros((count, PAD, CH), out_ref.dtype)
        for j in range(count):
            part = in_ref[j].astype(jnp.float32)
            part = jnp.where(degree >= first + j, part, 0.0)
            out_ref[j, :BAND, :DEG] = part.astype(out_ref.dtype)


def pass_kernel(in_ref, out_ref):
    for i in range(in_ref.shape[0]):
        out_ref[i] = in_ref[i]


def part_of(p):
    return pl.ds(pl.multiple_of(p * PART, 8), PART)


def dft_kernel(quad_ref, x_ref, t_ref, out_ref, s_ref):
    step = pl.program_id(0)
    x = jnp.concatenate(
        [x_ref[:, 0].reshape(LON * PAD, CH), x_ref[:, 1].reshape(LON * PAD, CH)], axis=1
    )
    rows = 1536

    @pl.loop(0, RM * ALL // rows)
    def _(chunk):
        t = t_ref[pl.ds(pl.multiple_of(chunk * rows, rows), rows), :]
        y = jnp.dot(t, x, preferred_element_type=jnp.float32)
        for j in range(2):
            a = 2 * step + j
            scaled = y[:, j * CH : (j + 1) * CH] * quad_ref[a]
            for k in range(rows // ALL):
                s_ref[pl.ds(a * RM + chunk * (rows // ALL) + k, ALL, stride=BLOCK), :] = scaled[
                    k * ALL : (k + 1) * ALL
                ]

    @pl.when(step == pl.num_programs(0) - 1)
    def _():
        widen(s_ref, out_ref, SPEC)


def legendre_kernel(src_ref, dest_ref, w_ref, *refs):
    legs, outs, (s_in, s_out) = refs[:LAT], refs[LAT:-2], refs[-2:]
    m = pl.program_id(0)

    @pl.when(m == 0)
    def _():
        widen(w_ref, s_in, SPEC)

    parts = []
    for s in range(LAT):
        base = src_ref[s] * (PAD * RM) + m
        parts.append(
            jnp.concatenate(
                [s_in[pl.ds(base + r * OWN, PAD, stride=RM), :] for r in range(2)], axis=1
            ).astype(jnp.bfloat16)
        )
    w = jnp.concatenate(parts, axis=0)
    leg = jnp.concatenate([leg_ref[0] for leg_ref in legs], axis=0)
    y = lax.dot_general(leg, w, (((0,), (0,)), ((), ())), preferred_element_type=jnp.float32)
    for r in range(2):
        s_out[pl.ds(r * OWN + m, DEG, stride=RM), :] = y[:DEG, r * CH : (r + 1) * CH]

    @pl.when(m == pl.num_programs(0) - 1)
    def _():
        for s, out_ref in enumerate(outs):
            out_ref[...] = s_out[part_of(dest_ref[s]), :].astype(out_ref.dtype)


def mix_kernel(*refs):
    n = (len(refs) - 4) // 2
    xs, (wr_ref, wi_ref), outs = refs[:n], refs[n : n + 2], refs[n + 2 : -2]
    s_in, s_out = refs[-2:]
    step = pl.program_id(0)

    @pl.when(step == 0)
    def _():
        for s, x_ref in enumerate(xs):
            s_in[part_of(s), :] = x_ref[...].astype(s_in.dtype)

    count = wr_ref.shape[0]
    for d in range(count):
        base = (step * count + d) * RM
        x = jnp.concatenate(
            [
                jnp.concatenate(
                    [s_in[pl.ds(base + r * OWN + j, n, stride=PART), :] for j in range(OWN)],
                    axis=0,
                )
                for r in range(2)
            ],
            axis=1,
        ).astype(jnp.bfloat16)
        wr, wi = wr_ref[d], wi_ref[d]
        w = jnp.concatenate(
            [jnp.concatenate([wr, wi], axis=1), jnp.concatenate([-wi, wr], axis=1)], axis=0
        )
        y = jnp.dot(x, w, preferred_element_type=jnp.float32)
        for r in range(2):
            for j in range(OWN):
                s_out[pl.ds(base + r * OWN + j, n, stride=PART), :] = y[
                    j * n : (j + 1) * n, r * CH : (r + 1) * CH
                ]

    @pl.when(step == pl.num_programs(0) - 1)
    def _():
        for s, out_ref in enumerate(outs):
            out_ref[...] = s_out[part_of(s), :].astype(out_ref.dtype)


def inverse_legendre_kernel(src_ref, dest_ref, *refs):
    xs, legs, (out_ref, s_in, s_out) = refs[:LAT], refs[LAT:-3], refs[-3:]
    m = pl.program_id(0)

    @pl.when(m == 0)
    def _():
        for s, x_ref in enumerate(xs):
            s_in[part_of(dest_ref[s]), :] = x_ref[...].astype(s_in.dtype)

    x = jnp.concatenate(
        [s_in[pl.ds(r * OWN + m, DEG, stride=RM), :] for r in range(2)], axis=1
    ).astype(jnp.bfloat16)
    x = jnp.concatenate([x, jnp.zeros((DEGPAD - DEG, 2 * CH), jnp.bfloat16)], axis=0)
    leg = jnp.concatenate([leg_ref[0] for leg_ref in legs], axis=0)
    y = jnp.dot(leg, x, preferred_element_type=jnp.float32)
    for s in range(LAT):
        base = src_ref[s] * (PAD * RM) + m
        for r in range(2):
            s_out[pl.ds(base + r * OWN, PAD, stride=RM), :] = y[
                s * PAD : (s + 1) * PAD, r * CH : (r + 1) * CH
            ]

    @pl.when(m == pl.num_programs(0) - 1)
    def _():
        widen(s_out, out_ref, SPEC)


def inverse_dft_kernel(x_ref, t_ref, out_ref, s_in):
    step = pl.program_id(0)

    @pl.when(step == 0)
    def _():
        widen(x_ref, s_in, SPEC)

    x = jnp.concatenate(
        [
            jnp.concatenate(
                [s_in[pl.ds((2 * step + j) * RM + k, ALL, stride=BLOCK), :] for k in range(RM)],
                axis=0,
            )
            for j in range(2)
        ],
        axis=1,
    ).astype(jnp.bfloat16)
    blocks = 16
    rows = blocks * PAD

    @pl.loop(0, LON // blocks)
    def _(chunk):
        t = t_ref[pl.ds(pl.multiple_of(chunk * rows, rows), rows), :]
        y = jnp.dot(t, x, preferred_element_type=jnp.float32).astype(jnp.bfloat16)
        for j in range(2):
            out_ref[pl.ds(chunk * blocks, blocks), j] = y[:, j * CH : (j + 1) * CH].reshape(
                blocks, PAD, CH
            )


def params(limit=VMEM):
    return pltpu.CompilerParams(dimension_semantics=("arbitrary",), vmem_limit_bytes=limit)


def whole(shape):
    return pl.BlockSpec(shape, lambda *_: (0,) * len(shape))


def cut(table, p, q, places):
    count, n = 3, len(places)
    return pl.pallas_call(
        functools.partial(cut_kernel, places),
        grid_spec=pltpu.PrefetchScalarGridSpec(
            num_scalar_prefetch=2,
            grid=(OWN // count,),
            in_specs=[
                pl.BlockSpec((count, BAND, DEG), lambda i, p, q, s=s: (block_of(p[0], s) + i, 0, 0))
                for s in places
            ],
            out_specs=[pl.BlockSpec((count, PAD, DEGPAD), lambda i, p, q: (i, 0, 0))] * n,
        ),
        out_shape=[jax.ShapeDtypeStruct((OWN, PAD, DEGPAD), jnp.bfloat16)] * n,
        compiler_params=params(CUT_VMEM),
        cost_estimate=pl.CostEstimate(
            flops=1_000_000 * n, bytes_accessed=1_700_000 * n, transcendentals=0
        ),
        name="cut",
    )(p.reshape(1), q.reshape(1), *[table] * n)


def in_order(token):
    return pl.pallas_call(
        pass_kernel,
        in_specs=[pl.BlockSpec(memory_space=pltpu.SMEM)],
        out_specs=pl.BlockSpec(memory_space=pltpu.SMEM),
        out_shape=jax.ShapeDtypeStruct(token.shape, token.dtype),
        compiler_params=pltpu.CompilerParams(vmem_limit_bytes=1024 * 1024),
        cost_estimate=pl.CostEstimate(
            flops=60_000_000_000, bytes_accessed=200_000_000, transcendentals=0
        ),
        name="in_order",
    )(token)


def dft(quad, x, table):
    return pl.pallas_call(
        dft_kernel,
        grid=(OWN // 2,),
        in_specs=[
            pl.BlockSpec(memory_space=pltpu.SMEM),
            pl.BlockSpec((LON, 2, PAD, CH), lambda s: (0, s, 0, 0)),
            whole((RM * ALL, LON * PAD)),
        ],
        out_specs=whole((SPEC, CH)),
        out_shape=jax.ShapeDtypeStruct((SPEC, CH), jnp.bfloat16),
        scratch_shapes=[pltpu.VMEM((SPEC, CH), jnp.float32)],
        compiler_params=params(),
        cost_estimate=pl.CostEstimate(
            flops=1_000_000, bytes_accessed=100_000, transcendentals=0
        ),
        name="dft",
    )(quad, x, table)


def legendre_call(kernel, name, src, dest, xs, legs, rows_out, limit):
    rows_in = [x.shape[0] for x in xs]
    return pl.pallas_call(
        kernel,
        grid=(OWN,),
        in_specs=[pl.BlockSpec(memory_space=pltpu.SMEM)] * 2
        + [whole((rows, CH)) for rows in rows_in]
        + [pl.BlockSpec((1, PAD, DEGPAD), lambda m: (m, 0, 0))] * LAT,
        out_specs=[whole((rows, CH)) for rows in rows_out],
        out_shape=[jax.ShapeDtypeStruct((rows, CH), jnp.bfloat16) for rows in rows_out],
        scratch_shapes=[
            pltpu.VMEM((sum(rows_in), CH), jnp.float32),
            pltpu.VMEM((sum(rows_out), CH), jnp.float32),
        ],
        compiler_params=params(limit),
        cost_estimate=pl.CostEstimate(
            flops=2 * 6 * 768 * 768 * 256, bytes_accessed=12_000_000, transcendentals=0
        ),
        name=name,
    )(src, dest, *xs, *legs)


def mix(xs, wr, wi):
    n = len(xs)
    weight = pl.BlockSpec((STEP, CH, CH), lambda s: (s, 0, 0))
    return pl.pallas_call(
        mix_kernel,
        grid=(BAND // STEP,),
        in_specs=[whole((PART, CH))] * n + [weight, weight],
        out_specs=[whole((PART, CH))] * n,
        out_shape=[jax.ShapeDtypeStruct((PART, CH), jnp.bfloat16)] * n,
        scratch_shapes=[pltpu.VMEM((n * PART, CH), jnp.float32)] * 2,
        compiler_params=params(),
        cost_estimate=pl.CostEstimate(
            flops=2 * 90 * 48 * 256 * 256, bytes_accessed=10_000_000, transcendentals=0
        ),
        name="mix",
    )(*xs, wr, wi)


def inverse_dft(x, table):
    return pl.pallas_call(
        inverse_dft_kernel,
        grid=(OWN // 2,),
        in_specs=[whole((SPEC, CH)), whole((LON * PAD, RM * ALL))],
        out_specs=pl.BlockSpec((LON, 2, PAD, CH), lambda s: (0, s, 0, 0)),
        out_shape=jax.ShapeDtypeStruct((LON, OWN, PAD, CH), jnp.bfloat16),
        scratch_shapes=[pltpu.VMEM((SPEC, CH), jnp.float32)],
        compiler_params=params(),
        cost_estimate=pl.CostEstimate(
            flops=2 * 1536 * 1536 * 768, bytes_accessed=10_000_000, transcendentals=0
        ),
        name="inverse_dft",
    )(x, table)


def swap(x, axes):
    return lax.all_to_all(x, axes, split_axis=0, concat_axis=0, tiled=True)


def shifted(part, shift):
    if shift == 0:
        return part
    return lax.ppermute(part, "lat", [(i, (i + shift) % LAT) for i in range(LAT)])


def per_device(field, legendre, quadrature, mix_real, mix_imag):
    p = lax.axis_index("lat")
    q = lax.axis_index("lon")
    forward_table, inverse_table = make_tables()

    rows = swap(jnp.pad(field, ((0, PAD - BAND), (0, PAD - BAND), (0, 0))), "lon")

    table = jnp.transpose(legendre, (0, 2, 1))
    shifts = jnp.array(SHIFTS, jnp.int32)
    src = lax.rem(p - shifts + LAT, LAT)
    dest = lax.rem(p + jnp.array(SENDS, jnp.int32), LAT)
    cuts = [None] * LAT
    for group in ((1, 2), (3, 4), (5, 6, 7, 0)):
        parts = cut(table, p, q, group)
        table, *parts = lax.optimization_barrier((table, *parts))
        for i, part in zip(group, parts):
            cuts[i] = part
    quad = lax.dynamic_slice_in_dim(jnp.pad(quadrature, (0, PAD - BAND)), q * OWN, OWN, 0)

    legs = list(cuts)

    def end(value, places):
        parts = [shifted(cuts[i], SHIFTS[i]) for i in places]
        value, parts = lax.optimization_barrier((value, parts))
        for i, part in zip(places, parts):
            legs[i] = part
        return value

    dest = in_order(end(dest, (1, 2, 3, 4, 7)))
    cuts[5:7], dest = lax.optimization_barrier((cuts[5:7], dest))
    rows, dest = lax.optimization_barrier((rows, dest))
    spectrum = dft(quad, rows.reshape(LON, OWN, PAD, CH), jnp.asarray(forward_table))
    dest = in_order(end(dest, (5, 6)))
    weighted = swap(spectrum, ("lat", "lon"))
    coefficients = legendre_call(
        legendre_kernel, "legendre", src, dest, [weighted], legs, [PART] * LAT, VMEM
    )
    mixed = []
    for group in GROUPS:
        parts = [shifted(coefficients[len(mixed) + i], shift) for i, shift in enumerate(group)]
        parts = mix(parts, mix_real, mix_imag)
        mixed += [shifted(part, (LAT - shift) % LAT) for part, shift in zip(parts, group)]
    (grid_spectrum,) = legendre_call(
        inverse_legendre_kernel, "inverse_legendre", src, dest, mixed, legs, [SPEC], VMEM
    )
    grid_spectrum = swap(grid_spectrum, ("lat", "lon"))
    samples = inverse_dft(grid_spectrum, jnp.asarray(inverse_table))
    synthesis = swap(samples.reshape(LON * OWN, PAD, CH), "lon")[:BAND, :BAND]
    return (field.astype(jnp.float32) + synthesis.astype(jnp.float32)).astype(jnp.bfloat16)


def solution(mesh):
    placed = (
        P("lat", "lon", None),
        P("lon", None, "lat"),
        P("lat"),
        P("lat", None, None),
        P("lat", None, None),
    )
    return jax.shard_map(
        per_device, mesh=mesh, in_specs=placed, out_specs=P("lat", "lon", None), check_vma=False
    )
```

```python
import functools

import jax
import jax.numpy as jnp
import ml_dtypes
import numpy as np
from jax import lax
from jax.experimental import pallas as pl
from jax.experimental.pallas import tpu as pltpu
from jax.sharding import PartitionSpec as P

LAT = 8
LON = 16
ALL = LAT * LON
BAND = 90
PAD = 96
OWN = 6
RM = 2 * OWN
BLOCK = OWN * RM
SPEC = ALL * BLOCK
DEG = 720
DEGPAD = 768
COEF = DEG * RM
PART = BAND * RM
STEP = 30
SHIFTS = (0, 1, 7, 2, 6, 3, 5, 4)
GROUPS = ((4, 3, 5), (2, 6, 1, 7, 0))
SENDS = GROUPS[0] + GROUPS[1]
CH = 128
FULL = 1440
VMEM = 24 * 1024 * 1024
CUT_VMEM = 58 * 1024 * 1024


def order_of():
    p = np.arange(LAT)[None, :, None]
    q = np.arange(LON)[None, None, :]
    j = np.arange(OWN)[:, None, None]
    first = np.minimum(6 * p, 45 - OWN)
    order = 45 * q + first + j
    valid = np.broadcast_to(first + j >= 6 * p, order.shape)
    return order.reshape(-1), valid.reshape(-1)


def make_tables():
    order, valid = order_of()
    n = np.arange(FULL)
    phase = (n[:, None] * order[None, :] % FULL).astype(np.float32) * np.float32(2.0 * np.pi / FULL)
    cosine = np.cos(phase.astype(np.float64)).astype(np.float32)
    sine = np.sin(phase.astype(np.float64)).astype(np.float32)
    both = np.concatenate([cosine, -sine], 1) * np.concatenate([valid, valid])[None, :]
    both = both.reshape(LON, BAND, 2 * OWN * ALL)
    both = np.pad(both, ((0, 0), (0, PAD - BAND), (0, 0))).reshape(LON * PAD, RM * ALL)
    forward = both * np.float32(1.0 / np.sqrt(np.float32(FULL)))
    inverse = both * np.sqrt(np.float32(2.0 / FULL))
    return (
        np.ascontiguousarray(forward.T).astype(ml_dtypes.bfloat16),
        np.ascontiguousarray(inverse).astype(ml_dtypes.bfloat16),
    )


def widen(src, dst, rows):
    step = 576

    @pl.loop(0, rows // step)
    def _(i):
        part = pl.ds(pl.multiple_of(i * step, step), step)
        dst[part, :] = src[part, :].astype(dst.dtype)


def block_of(p, s):
    return jnp.minimum(lax.rem(p + SHIFTS[s], LAT) * (OWN // 3), 45 // 3 - OWN // 3)


def cut_kernel(places, p_ref, q_ref, *refs):
    ins, outs = refs[: len(refs) // 2], refs[len(refs) // 2 :]
    count = ins[0].shape[0]
    degree = lax.broadcasted_iota(jnp.int32, (BAND, DEG), 1)
    for s, in_ref, out_ref in zip(places, ins, outs):
        first = q_ref[0] * 45 + (block_of(p_ref[0], s) + pl.program_id(0)) * count
        out_ref[:, PAD - 16 :, :] = jnp.zeros((count, 16, DEGPAD), out_ref.dtype)
        out_ref[:, :, DEGPAD - CH :] = jnp.zeros((count, PAD, CH), out_ref.dtype)
        for j in range(count):
            part = in_ref[j].astype(jnp.float32)
            part = jnp.where(degree >= first + j, part, 0.0)
            out_ref[j, :BAND, :DEG] = part.astype(out_ref.dtype)


def pass_kernel(in_ref, out_ref):
    for i in range(in_ref.shape[0]):
        out_ref[i] = in_ref[i]


def part_of(p):
    return pl.ds(pl.multiple_of(p * PART, 8), PART)


def dft_kernel(quad_ref, x_ref, t_ref, out_ref, s_ref):
    step = pl.program_id(0)
    x = jnp.concatenate(
        [x_ref[:, 0].reshape(LON * PAD, CH), x_ref[:, 1].reshape(LON * PAD, CH)], axis=1
    )
    rows = 1536

    @pl.loop(0, RM * ALL // rows)
    def _(chunk):
        t = t_ref[pl.ds(pl.multiple_of(chunk * rows, rows), rows), :]
        y = jnp.dot(t, x, preferred_element_type=jnp.float32)
        for j in range(2):
            a = 2 * step + j
            scaled = y[:, j * CH : (j + 1) * CH] * quad_ref[a]
            for k in range(rows // ALL):
                s_ref[pl.ds(a * RM + chunk * (rows // ALL) + k, ALL, stride=BLOCK), :] = scaled[
                    k * ALL : (k + 1) * ALL
                ]

    @pl.when(step == pl.num_programs(0) - 1)
    def _():
        widen(s_ref, out_ref, SPEC)


def legendre_kernel(src_ref, dest_ref, w_ref, *refs):
    legs, outs, (s_in, s_out) = refs[:LAT], refs[LAT:-2], refs[-2:]
    m = pl.program_id(0)

    @pl.when(m == 0)
    def _():
        widen(w_ref, s_in, SPEC)

    parts = []
    for s in range(LAT):
        base = src_ref[s] * (PAD * RM) + m
        parts.append(
            jnp.concatenate(
                [s_in[pl.ds(base + r * OWN, PAD, stride=RM), :] for r in range(2)], axis=1
            ).astype(jnp.bfloat16)
        )
    w = jnp.concatenate(parts, axis=0)
    leg = jnp.concatenate([leg_ref[0] for leg_ref in legs], axis=0)
    y = lax.dot_general(leg, w, (((0,), (0,)), ((), ())), preferred_element_type=jnp.float32)
    for r in range(2):
        s_out[pl.ds(r * OWN + m, DEG, stride=RM), :] = y[:DEG, r * CH : (r + 1) * CH]

    @pl.when(m == pl.num_programs(0) - 1)
    def _():
        for s, out_ref in enumerate(outs):
            out_ref[...] = s_out[part_of(dest_ref[s]), :].astype(out_ref.dtype)


def mix_kernel(*refs):
    n = (len(refs) - 4) // 2
    xs, (wr_ref, wi_ref), outs = refs[:n], refs[n : n + 2], refs[n + 2 : -2]
    s_in, s_out = refs[-2:]
    step = pl.program_id(0)

    @pl.when(step == 0)
    def _():
        for s, x_ref in enumerate(xs):
            s_in[part_of(s), :] = x_ref[...].astype(s_in.dtype)

    count = wr_ref.shape[0]
    for d in range(count):
        base = (step * count + d) * RM
        x = jnp.concatenate(
            [
                jnp.concatenate(
                    [s_in[pl.ds(base + r * OWN + j, n, stride=PART), :] for j in range(OWN)],
                    axis=0,
                )
                for r in range(2)
            ],
            axis=1,
        ).astype(jnp.bfloat16)
        wr, wi = wr_ref[d], wi_ref[d]
        w = jnp.concatenate(
            [jnp.concatenate([wr, wi], axis=1), jnp.concatenate([-wi, wr], axis=1)], axis=0
        )
        y = jnp.dot(x, w, preferred_element_type=jnp.float32)
        for r in range(2):
            for j in range(OWN):
                s_out[pl.ds(base + r * OWN + j, n, stride=PART), :] = y[
                    j * n : (j + 1) * n, r * CH : (r + 1) * CH
                ]

    @pl.when(step == pl.num_programs(0) - 1)
    def _():
        for s, out_ref in enumerate(outs):
            out_ref[...] = s_out[part_of(s), :].astype(out_ref.dtype)


def inverse_legendre_kernel(src_ref, dest_ref, *refs):
    xs, legs, (out_ref, s_in, s_out) = refs[:LAT], refs[LAT:-3], refs[-3:]
    m = pl.program_id(0)

    @pl.when(m == 0)
    def _():
        for s, x_ref in enumerate(xs):
            s_in[part_of(dest_ref[s]), :] = x_ref[...].astype(s_in.dtype)

    x = jnp.concatenate(
        [s_in[pl.ds(r * OWN + m, DEG, stride=RM), :] for r in range(2)], axis=1
    ).astype(jnp.bfloat16)
    x = jnp.concatenate([x, jnp.zeros((DEGPAD - DEG, 2 * CH), jnp.bfloat16)], axis=0)
    leg = jnp.concatenate([leg_ref[0] for leg_ref in legs], axis=0)
    y = jnp.dot(leg, x, preferred_element_type=jnp.float32)
    for s in range(LAT):
        base = src_ref[s] * (PAD * RM) + m
        for r in range(2):
            s_out[pl.ds(base + r * OWN, PAD, stride=RM), :] = y[
                s * PAD : (s + 1) * PAD, r * CH : (r + 1) * CH
            ]

    @pl.when(m == pl.num_programs(0) - 1)
    def _():
        widen(s_out, out_ref, SPEC)


def inverse_dft_kernel(x_ref, t_ref, out_ref, s_in):
    step = pl.program_id(0)

    @pl.when(step == 0)
    def _():
        widen(x_ref, s_in, SPEC)

    x = jnp.concatenate(
        [
            jnp.concatenate(
                [s_in[pl.ds((2 * step + j) * RM + k, ALL, stride=BLOCK), :] for k in range(RM)],
                axis=0,
            )
            for j in range(2)
        ],
        axis=1,
    ).astype(jnp.bfloat16)
    blocks = 16
    rows = blocks * PAD

    @pl.loop(0, LON // blocks)
    def _(chunk):
        t = t_ref[pl.ds(pl.multiple_of(chunk * rows, rows), rows), :]
        y = jnp.dot(t, x, preferred_element_type=jnp.float32).astype(jnp.bfloat16)
        for j in range(2):
            out_ref[pl.ds(chunk * blocks, blocks), j] = y[:, j * CH : (j + 1) * CH].reshape(
                blocks, PAD, CH
            )


def params(limit=VMEM):
    return pltpu.CompilerParams(dimension_semantics=("arbitrary",), vmem_limit_bytes=limit)


def whole(shape):
    return pl.BlockSpec(shape, lambda *_: (0,) * len(shape))


def cut(table, p, q, places):
    count, n = 3, len(places)
    return pl.pallas_call(
        functools.partial(cut_kernel, places),
        grid_spec=pltpu.PrefetchScalarGridSpec(
            num_scalar_prefetch=2,
            grid=(OWN // count,),
            in_specs=[
                pl.BlockSpec((count, BAND, DEG), lambda i, p, q, s=s: (block_of(p[0], s) + i, 0, 0))
                for s in places
            ],
            out_specs=[pl.BlockSpec((count, PAD, DEGPAD), lambda i, p, q: (i, 0, 0))] * n,
        ),
        out_shape=[jax.ShapeDtypeStruct((OWN, PAD, DEGPAD), jnp.bfloat16)] * n,
        compiler_params=params(CUT_VMEM),
        cost_estimate=pl.CostEstimate(
            flops=1_000_000 * n, bytes_accessed=1_700_000 * n, transcendentals=0
        ),
        name="cut",
    )(p.reshape(1), q.reshape(1), *[table] * n)


def in_order(token):
    return pl.pallas_call(
        pass_kernel,
        in_specs=[pl.BlockSpec(memory_space=pltpu.SMEM)],
        out_specs=pl.BlockSpec(memory_space=pltpu.SMEM),
        out_shape=jax.ShapeDtypeStruct(token.shape, token.dtype),
        compiler_params=pltpu.CompilerParams(vmem_limit_bytes=1024 * 1024),
        cost_estimate=pl.CostEstimate(
            flops=60_000_000_000, bytes_accessed=200_000_000, transcendentals=0
        ),
        name="in_order",
    )(token)


def dft(quad, x, table):
    return pl.pallas_call(
        dft_kernel,
        grid=(OWN // 2,),
        in_specs=[
            pl.BlockSpec(memory_space=pltpu.SMEM),
            pl.BlockSpec((LON, 2, PAD, CH), lambda s: (0, s, 0, 0)),
            whole((RM * ALL, LON * PAD)),
        ],
        out_specs=whole((SPEC, CH)),
        out_shape=jax.ShapeDtypeStruct((SPEC, CH), jnp.bfloat16),
        scratch_shapes=[pltpu.VMEM((SPEC, CH), jnp.float32)],
        compiler_params=params(),
        cost_estimate=pl.CostEstimate(
            flops=1_000_000, bytes_accessed=100_000, transcendentals=0
        ),
        name="dft",
    )(quad, x, table)


def legendre_call(kernel, name, src, dest, xs, legs, rows_out, limit):
    rows_in = [x.shape[0] for x in xs]
    return pl.pallas_call(
        kernel,
        grid=(OWN,),
        in_specs=[pl.BlockSpec(memory_space=pltpu.SMEM)] * 2
        + [whole((rows, CH)) for rows in rows_in]
        + [pl.BlockSpec((1, PAD, DEGPAD), lambda m: (m, 0, 0))] * LAT,
        out_specs=[whole((rows, CH)) for rows in rows_out],
        out_shape=[jax.ShapeDtypeStruct((rows, CH), jnp.bfloat16) for rows in rows_out],
        scratch_shapes=[
            pltpu.VMEM((sum(rows_in), CH), jnp.float32),
            pltpu.VMEM((sum(rows_out), CH), jnp.float32),
        ],
        compiler_params=params(limit),
        cost_estimate=pl.CostEstimate(
            flops=2 * 6 * 768 * 768 * 256, bytes_accessed=12_000_000, transcendentals=0
        ),
        name=name,
    )(src, dest, *xs, *legs)


def mix(xs, wr, wi):
    n = len(xs)
    weight = pl.BlockSpec((STEP, CH, CH), lambda s: (s, 0, 0))
    return pl.pallas_call(
        mix_kernel,
        grid=(BAND // STEP,),
        in_specs=[whole((PART, CH))] * n + [weight, weight],
        out_specs=[whole((PART, CH))] * n,
        out_shape=[jax.ShapeDtypeStruct((PART, CH), jnp.bfloat16)] * n,
        scratch_shapes=[pltpu.VMEM((n * PART, CH), jnp.float32)] * 2,
        compiler_params=params(),
        cost_estimate=pl.CostEstimate(
            flops=2 * 90 * 48 * 256 * 256, bytes_accessed=10_000_000, transcendentals=0
        ),
        name="mix",
    )(*xs, wr, wi)


def inverse_dft(x, table):
    return pl.pallas_call(
        inverse_dft_kernel,
        grid=(OWN // 2,),
        in_specs=[whole((SPEC, CH)), whole((LON * PAD, RM * ALL))],
        out_specs=pl.BlockSpec((LON, 2, PAD, CH), lambda s: (0, s, 0, 0)),
        out_shape=jax.ShapeDtypeStruct((LON, OWN, PAD, CH), jnp.bfloat16),
        scratch_shapes=[pltpu.VMEM((SPEC, CH), jnp.float32)],
        compiler_params=params(),
        cost_estimate=pl.CostEstimate(
            flops=2 * 1536 * 1536 * 768, bytes_accessed=10_000_000, transcendentals=0
        ),
        name="inverse_dft",
    )(x, table)


def swap(x, axes):
    return lax.all_to_all(x, axes, split_axis=0, concat_axis=0, tiled=True)


def shifted(part, shift):
    if shift == 0:
        return part
    return lax.ppermute(part, "lat", [(i, (i + shift) % LAT) for i in range(LAT)])


def per_device(field, legendre, quadrature, mix_real, mix_imag):
    p = lax.axis_index("lat")
    q = lax.axis_index("lon")
    forward_table, inverse_table = make_tables()

    rows = swap(jnp.pad(field, ((0, PAD - BAND), (0, PAD - BAND), (0, 0))), "lon")

    table = jnp.transpose(legendre, (0, 2, 1))
    shifts = jnp.array(SHIFTS, jnp.int32)
    src = lax.rem(p - shifts + LAT, LAT)
    dest = lax.rem(p + jnp.array(SENDS, jnp.int32), LAT)
    cuts = [None] * LAT
    for group in ((1, 2), (3, 4), (7,), (5, 6, 0)):
        parts = cut(table, p, q, group)
        table, *parts = lax.optimization_barrier((table, *parts))
        for i, part in zip(group, parts):
            cuts[i] = part
    quad = lax.dynamic_slice_in_dim(jnp.pad(quadrature, (0, PAD - BAND)), q * OWN, OWN, 0)

    legs = list(cuts)

    def end(value, places):
        parts = [shifted(cuts[i], SHIFTS[i]) for i in places]
        value, parts = lax.optimization_barrier((value, parts))
        for i, part in zip(places, parts):
            legs[i] = part
        return value

    dest = end(dest, (1, 2, 3, 4, 7))
    cuts[5:7], dest = lax.optimization_barrier((cuts[5:7], dest))
    dest = in_order(dest)
    rows, dest = lax.optimization_barrier((rows, dest))
    spectrum = dft(quad, rows.reshape(LON, OWN, PAD, CH), jnp.asarray(forward_table))
    dest = in_order(end(dest, (5, 6)))
    weighted = swap(spectrum, ("lat", "lon"))
    coefficients = legendre_call(
        legendre_kernel, "legendre", src, dest, [weighted], legs, [PART] * LAT, VMEM
    )
    mixed = []
    for group in GROUPS:
        parts = [shifted(coefficients[len(mixed) + i], shift) for i, shift in enumerate(group)]
        parts = mix(parts, mix_real, mix_imag)
        mixed += [shifted(part, (LAT - shift) % LAT) for part, shift in zip(parts, group)]
    (grid_spectrum,) = legendre_call(
        inverse_legendre_kernel, "inverse_legendre", src, dest, mixed, legs, [SPEC], VMEM
    )
    grid_spectrum = swap(grid_spectrum, ("lat", "lon"))
    samples = inverse_dft(grid_spectrum, jnp.asarray(inverse_table))
    synthesis = swap(samples.reshape(LON * OWN, PAD, CH), "lon")[:BAND, :BAND]
    return (field.astype(jnp.float32) + synthesis.astype(jnp.float32)).astype(jnp.bfloat16)


def solution(mesh):
    placed = (
        P("lat", "lon", None),
        P("lon", None, "lat"),
        P("lat"),
        P("lat", None, None),
        P("lat", None, None),
    )
    return jax.shard_map(
        per_device, mesh=mesh, in_specs=placed, out_specs=P("lat", "lon", None), check_vma=False
    )
```
